256 devices in a mesh: dp: 64 (over z, x, core), rep: 4 (over y).
Axes of the slice: x: 4, y: 4, z: 8, core: 2. Of those that a mesh axis runs over, the one named last changes fastest.
Arguments:
- hot_slab: bfloat16 [32768, 128], replicated, may hold values from -3 to 3
- hot_accum: float32 [32768], P(('dp', 'rep')), may hold values from 0.001 to 0.1
- cold_table: float32 [131072, 128], P('dp'), may hold values from -3 to 3
- cold_accum: float32 [131072], P('dp'), may hold values from 0.0001 to 0.01
- touched_owner: int32 [262144, 1], P(('dp', 'rep')), may hold values from 0 to 63; in each aligned block of 1024 rows (0 to 1023, 1024 to 2047, ...) at most 48 rows name the same one
- touched_row: int32 [262144], P(('dp', 'rep')), may hold values from 0 to 2047
- lookup_index: int32 [2097152], P(('dp', 'rep')), may hold values from 0 to 33791
- bag_id: int32 [256, 8192], P(('dp', 'rep')), may hold values from 0 to 2047, never falling along the last dimension, each value on 1 to 16 neighbouring positions
- labels: float32 [65536], P(('dp', 'rep')), may hold values from 0 to 1
- w_hidden: bfloat16 [1024, 1024], replicated, may hold values from -0.1875 to 0.1875
- hidden_accum: float32 [1024, 1024], P(('dp', 'rep')), may hold values from 1 to 30
- w_out: float32 [1024], replicated, may hold values from -0.1875 to 0.1875
- out_accum: float32 [1024], P(('dp', 'rep')), may hold values from 1000 to 30000
Outputs:
- hot_new: float32 [32768, 128], P(('dp', 'rep'))
- hot_accum_new: float32 [32768], P(('dp', 'rep'))
- cold_new: float32 [131072, 128], P('dp')
- cold_accum_new: float32 [131072], P('dp')
- hidden_new: float32 [1024, 1024], P(('dp', 'rep'))
- hidden_accum_new: float32 [1024, 1024], P(('dp', 'rep'))
- out_new: float32 [1024], P(('dp', 'rep'))
- out_accum_new: float32 [1024], P(('dp', 'rep'))
The draws below stay inside these ranges and needn't reach their ends.
Inputs may be any that keep to these rules, and one draw needn't show every extreme that they name: `touched_owner`: among the 1024 touched rows of one device, no owner is named more than 48 times. `bag_id`: Non-decreasing along each device's lookups; each of the 2048 bags holds 1 to 16 lookups.
All inputs are finite; a program needn't handle non-finite values.
Results may differ from the reference program's by a relative error of at most 0.00035.
Values may be sent and summed in bfloat16 or wider, within the bound.
No kernel may reach another device: no remote copies, remote signals or barrier semaphores. Data moves between devices by JAX's collectives and lax.ppermute only.
A program may use at most 128 MiB of HBM per device.

```python
import math
import jax
import jax.numpy as jnp
import numpy as np
from jax import lax

EMB = 128
HOT = 32768
INPUT = 1024
HID = 1024
B_DEV = 256
BAGS = 2048
LOOK = 8192
BAG_MOST = 16
UNIQ = 1024
CAP = 48
R_OWN = 2048
SAMPLES = 65536
N_DP = 64
DEVICES = 256


def plant(values, rng, least, largest):
    extent = values.shape
    spot = [jax.random.randint(jax.random.fold_in(rng, axis), (), 0, extent[axis]) for axis in range(len(extent))]
    values = values.at[tuple(spot)].set(least)
    longest = extent.index(max(extent))
    spot[longest] = (spot[longest] + 1) % extent[longest]
    return values.at[tuple(spot)].set(largest)


def levels(stream_key, dims, cuts, smallest, largest):
    level, own = 1.0, jax.random.fold_in(stream_key, 6)
    for axis_at, shards_of in cuts:
        heights = jnp.exp(jax.random.uniform(jax.random.fold_in(own, axis_at), (shards_of,), jnp.float32, smallest / len(cuts), largest / len(cuts)))
        level = level * jnp.repeat(heights, dims[axis_at] // shards_of).reshape([-1 if axis == axis_at else 1 for axis in range(len(dims))])
    return level


def rank_bounds(count, slope):
    weights = [(1 << 20) // math.isqrt(rank ** slope) + 1 for rank in range(1, count + 1)]
    spread = 1 + sum(weights) // (1 << 30)
    return np.cumsum(np.array([max(1, weight // spread) for weight in weights]))


def ranked_ids(key, extent, number_of, slope):
    table = rank_bounds(number_of, slope)
    lot = jax.random.randint(jax.random.fold_in(key, 1), extent, 0, int(table[number_of - 1]))
    standing = jnp.searchsorted(jnp.asarray(table, jnp.int32), lot, side="right")
    return jax.random.permutation(jax.random.fold_in(key, 2), number_of)[standing].astype(jnp.int32)


def profile(number_of, total, reach, skew):
    loads = [(1 << 20) // math.isqrt(grade ** skew) + 1 for grade in range(2, number_of + 1)]
    rest, holding = total - reach - (number_of - 1), [1] * (number_of - 1)
    while rest > 0:
        free = [i for i in range(number_of - 1) if holding[i] < reach]
        mass, budget = sum([loads[i] for i in free]), rest
        for i in free:
            extra = min(reach - holding[i], max(1, budget * loads[i] // mass), rest)
            holding[i] = holding[i] + extra
            rest = rest - extra
    return np.array([reach] + holding)


def uneven_parts(rng, count, total, bound, lean):
    if count == 2:
        one = jax.random.randint(rng, (), max(1, total - bound), min(bound, total - 1) + 1)
        return jnp.stack([one, total - one])
    tallies = jnp.asarray(profile(count, total, bound, lean), jnp.int32)
    twos = (count - 1) // 2
    donor, taker = tallies[1:1 + 2 * twos:2], tallies[2:2 + 2 * twos:2]
    room = jnp.minimum(donor - 1, bound - taker)
    moved = jax.random.randint(jax.random.fold_in(rng, 1), (twos,), 0, 1 << 20) % (room + 1)
    tallies = tallies.at[1:1 + 2 * twos:2].set(donor - moved).at[2:2 + 2 * twos:2].set(taker + moved)
    return tallies[jax.random.permutation(jax.random.fold_in(rng, 2), count)]


def routed_block(rng, own, number, rows, amount, top, reach, slope):
    sequence = jax.random.permutation(rng, amount)
    crowded, usual = portions_of(amount, rows * top, reach, slope, True), portions_of(amount, rows * top, reach, slope, False)
    places = jnp.arange(amount)

    def named(tallies, turn):
        used = int((tallies > 0).sum())
        fixed = max(1, used // 4)
        shifted = fixed + (places - fixed + turn * (used - fixed)) % max(1, amount - fixed)
        return jnp.zeros((amount,), jnp.int32).at[sequence[jnp.where(places < fixed, places, shifted)]].set(jnp.asarray(tallies, jnp.int32))

    tallies = jnp.where(number % 4 == 0, named(crowded, number // 4), named(usual, number - number // 4 - 1))
    mixed = jax.random.permutation(jax.random.fold_in(own, 3), amount)
    source_of, sink = mixed[0:amount // 2 * 2:2], mixed[1:amount // 2 * 2:2]
    room = jnp.minimum(tallies[source_of] - 1, reach - tallies[sink]) // 2
    room = jnp.where((source_of == sequence[0]) | (sink == sequence[0]) | (tallies[sink] == 0), 0, jnp.maximum(room, 0))
    shifted = jax.random.randint(jax.random.fold_in(own, 4), (amount // 2,), 0, 1 << 20) % (room + 1)
    tallies = tallies.at[source_of].add(-shifted).at[sink].add(shifted)
    items = jnp.searchsorted(jnp.cumsum(tallies), jnp.arange(rows * top), side="right").astype(jnp.int32)
    listing = items.reshape(top, rows).T
    listing = listing[jax.random.permutation(jax.random.fold_in(own, 1), rows)]
    turn = jax.random.randint(jax.random.fold_in(own, 2), (rows, 1), 0, top)
    return jnp.take_along_axis(listing, (jnp.arange(top)[None, :] + turn) % top, axis=1)


def portions_of(count, total, reach, slope, full):
    portions = [(1 << 20) // math.isqrt(standing ** slope) + 1 for standing in range(1, count + 1)]
    largest = reach if full else min(reach, max(-(-total // count), total * portions[0] // sum(portions)))
    least = 1 if total - largest >= count - 1 else 0
    given, rest = [largest] + [least] * (count - 1), total - largest - least * (count - 1)
    while rest > 0:
        movable = [i for i in range(1, count) if given[i] < largest] or [i for i in range(1, count) if given[i] < reach]
        pool, budget = sum([portions[i] for i in movable]), rest
        for i in movable:
            addition = min(reach - given[i], max(1, budget * portions[i] // pool), rest)
            given[i] = given[i] + addition
            rest = rest - addition
    return np.array(given)


def bell_draw(rng, extent, deviation, limit, shards=(), held_as=jnp.bfloat16):
    drawn = jax.random.normal(rng, extent, jnp.float32) * deviation
    if len(shards) > 0:
        drawn = levels(rng, extent, shards, -0.22, 0.18) * drawn
    return jnp.clip(drawn, min=-limit, max=limit).astype(held_as)


def setup_inputs(seed: int = 0) -> dict:
    arg_keys = jax.random.split(jax.random.key(seed), 14)
    hot_slab = bell_draw(arg_keys[0], (HOT, EMB), 0.5, 3.0)
    hot_accum = jnp.clip(jnp.exp(math.log(0.1) - 4.6051702 * jax.random.uniform(arg_keys[1], (HOT,), jnp.float32) ** levels(arg_keys[1], (HOT,), ((0, 256),), -0.2, 0.2)), 0.001, 0.1)
    cold_table = bell_draw(arg_keys[2], (N_DP * R_OWN, EMB), 0.5, 3.0, ((0, 64),), jnp.float32)
    cold_accum = jnp.clip(jnp.exp(math.log(0.01) - 4.6051702 * jax.random.uniform(arg_keys[3], (N_DP * R_OWN,), jnp.float32) ** levels(arg_keys[3], (N_DP * R_OWN,), ((0, 64),), -0.2, 0.2)), 0.0001, 0.01)
    touched_owner_keys = jax.random.split(jax.random.fold_in(arg_keys[4], 1), (DEVICES * UNIQ) // UNIQ)
    touched_owner_turns = jax.random.permutation(jax.random.fold_in(arg_keys[4], 3), (DEVICES * UNIQ) // UNIQ)
    touched_owner = jax.vmap(lambda own, number: routed_block(jax.random.fold_in(arg_keys[4], 2), own, number, UNIQ, N_DP, 1, CAP, 2))(touched_owner_keys, touched_owner_turns).reshape((DEVICES * UNIQ, 1))
    touched_row = plant(jax.random.randint(arg_keys[5], (DEVICES * UNIQ,), 0, R_OWN), jax.random.fold_in(arg_keys[5], 1), 0, R_OWN - 1).astype(jnp.int32)
    lookup_index = plant(ranked_ids(arg_keys[6], (DEVICES * LOOK,), HOT + UNIQ, 1), jax.random.fold_in(arg_keys[6], 3), 0, (HOT + UNIQ) - 1).astype(jnp.int32)
    bag_id = jax.vmap(lambda own: jnp.searchsorted(jnp.cumsum(uneven_parts(own, BAGS, LOOK, BAG_MOST, 1)), jnp.arange(LOOK), side="right"))(jax.random.split(arg_keys[7], DEVICES)).reshape((DEVICES, LOOK)).astype(jnp.int32)
    labels = jnp.clip(1.0 * jax.random.uniform(arg_keys[8], (SAMPLES,), jnp.float32) ** levels(arg_keys[8], (SAMPLES,), ((0, 256),), -0.2, 0.2), 0.0, 1.0)
    w_hidden = bell_draw(arg_keys[9], (INPUT, HID), INPUT ** -0.5, 0.1875)
    hidden_accum = jnp.clip(jnp.exp(math.log(30.0) - 3.4011974 * jax.random.uniform(arg_keys[10], (INPUT, HID), jnp.float32) ** levels(arg_keys[10], (INPUT, HID), ((0, 256),), -0.2, 0.2)), 1.0, 30.0)
    w_out = bell_draw(arg_keys[11], (HID,), HID ** -0.5, 0.1875, (), jnp.float32)
    out_accum = jnp.clip(jnp.exp(math.log(30000.0) - 3.4011974 * jax.random.uniform(arg_keys[12], (HID,), jnp.float32) ** levels(arg_keys[12], (HID,), ((0, 256),), -0.2, 0.2)), 1000.0, 30000.0)
    return dict(hot_slab=hot_slab, hot_accum=hot_accum, cold_table=cold_table, cold_accum=cold_accum, touched_owner=touched_owner, touched_row=touched_row, lookup_index=lookup_index, bag_id=bag_id, labels=labels, w_hidden=w_hidden, hidden_accum=hidden_accum, w_out=w_out, out_accum=out_accum)


learn_rate = 0.05

def local_pass(hot_slab, fetched, lookups, bag_ids, targets, w_hidden, w_out):
    hot_count, emb_width = hot_slab.shape
    samples = targets.shape[0]
    input_width = w_hidden.shape[0]
    bag_count = samples * input_width // emb_width
    is_hot = lookups < hot_count
    hot_part = jnp.take(hot_slab, jnp.where(is_hot, lookups, 0), axis=0)
    cold_part = jnp.take(fetched, jnp.where(is_hot, 0, lookups - hot_count), axis=0)
    values = jnp.where(is_hot[:, None], hot_part, cold_part).astype(jnp.float32)
    pooled = jax.ops.segment_sum(values, bag_ids, num_segments=bag_count, indices_are_sorted=True)
    pooled_in = pooled.reshape(samples, input_width).astype(jnp.bfloat16)
    preact = jnp.dot(pooled_in, w_hidden, preferred_element_type=jnp.float32)
    gate_sig = jax.nn.sigmoid(preact)
    hidden_act = (preact * gate_sig).astype(jnp.bfloat16)
    act_wide = hidden_act.astype(jnp.float32)
    logits = jnp.dot(act_wide, w_out, precision=lax.Precision.HIGHEST)
    logit_grad = jax.nn.sigmoid(logits) - targets
    out_grad = jnp.dot(logit_grad, act_wide, precision=lax.Precision.HIGHEST)
    act_grad = (logit_grad[:, None] * w_out[None, :] * gate_sig * (1.0 + preact * (1.0 - gate_sig))).astype(jnp.bfloat16)
    hidden_grad = jnp.dot(pooled_in.T, act_grad, preferred_element_type=jnp.float32)
    input_grad = jnp.dot(act_grad, w_hidden.T, preferred_element_type=jnp.float32)
    lookup_grad = jnp.take(input_grad.reshape(bag_count, emb_width), bag_ids, axis=0)
    return (lookup_grad, is_hot, hidden_grad, out_grad)

def row_adagrad(param, accum, grad):
    accum_new = accum + lax.optimization_barrier(jnp.mean(grad * grad, axis=1))
    return (param - learn_rate * grad / jnp.sqrt(accum_new)[:, None], accum_new)

def elem_adagrad(param, accum, grad):
    accum_new = accum + grad * grad
    return (param - learn_rate * grad / jnp.sqrt(accum_new), accum_new)

def reference(hot_slab, hot_accum, cold_table, cold_accum, touched_owner, touched_row, lookup_index, bag_id, labels, w_hidden, hidden_accum, w_out, out_accum):
    emb_width = hot_slab.shape[1]
    owner_ids = touched_owner.reshape(DEVICES, UNIQ)
    row_ids = touched_row.reshape(DEVICES, UNIQ)
    lookups = lookup_index.reshape(DEVICES, LOOK)
    targets = labels.reshape(DEVICES, B_DEV)

    def one_device(totals, pieces):
        hot_total, cold_total, hidden_total, out_total = totals
        owner_row, local_row, device_lookups, device_bags, device_targets = pieces
        table_row = (owner_row * R_OWN + local_row).astype(jnp.int32)
        fetched = jnp.take(cold_table, table_row, axis=0).astype(jnp.bfloat16)
        lookup_grad, is_hot, hidden_grad, out_grad = local_pass(hot_slab, fetched, device_lookups, device_bags, device_targets, w_hidden, w_out)
        hot_target = jnp.where(is_hot, device_lookups, HOT).astype(jnp.int32)
        hot_total = hot_total.at[hot_target].add(lookup_grad, mode='drop')
        slot_target = jnp.where(is_hot, UNIQ, device_lookups - HOT).astype(jnp.int32)
        slot_grad = jnp.zeros((UNIQ, emb_width), jnp.float32).at[slot_target].add(lookup_grad, mode='drop')
        cold_total = cold_total.at[table_row].add(slot_grad)
        return ((hot_total, cold_total, hidden_total + hidden_grad, out_total + out_grad), None)
    start = (jnp.zeros((HOT, emb_width), jnp.float32), jnp.zeros((N_DP * R_OWN, emb_width), jnp.float32), jnp.zeros((INPUT, HID), jnp.float32), jnp.zeros((HID,), jnp.float32))
    totals, ignored = lax.scan(one_device, start, (owner_ids[:, :, 0] if owner_ids.ndim == 3 else owner_ids, row_ids, lookups, bag_id, targets))
    hot_grad, cold_grad, hidden_grad, out_grad = totals
    hot_new, hot_accum_new = row_adagrad(hot_slab.astype(jnp.float32), hot_accum, hot_grad)
    cold_new, cold_accum_new = row_adagrad(cold_table, cold_accum, cold_grad)
    hidden_new, hidden_accum_new = elem_adagrad(w_hidden.astype(jnp.float32), hidden_accum, hidden_grad)
    out_new, out_accum_new = elem_adagrad(w_out, out_accum, out_grad)
    return (hot_new, hot_accum_new, cold_new, cold_accum_new, hidden_new, hidden_accum_new, out_new, out_accum_new)
```

```python
import jax
import jax.numpy as jnp
from jax import lax
from jax.experimental import pallas as pl
from jax.experimental.pallas import tpu as pltpu
from jax.sharding import PartitionSpec as P

learn_rate = 0.05
bf16 = jnp.bfloat16
f32 = jnp.float32
i32 = jnp.int32

EMB = 128
HOT = 32768
FEAT = 8
HID = 1024
B_DEV = 256
BAGS = 2048
LOOK = 8192
UNIQ = 1024
CAP = 48
R_OWN = 2048
N_DP = 64
SLOTS = N_DP * CAP
GROUP = 16
BLOCK = 256
WINDOW = BLOCK + 16
BLOCKS = LOOK // BLOCK
BATCH = 4
PADDED = BAGS + WINDOW
MIB = 1 << 20

ORDERS = ((3, 2, 1, 0), (2, 3, 0, 1), (1, 0, 3, 2), (0, 1, 2, 3))

SMEM = pl.BlockSpec(memory_space=pltpu.SMEM)
VMEM = pl.BlockSpec(memory_space=pltpu.VMEM)
HBM = pl.BlockSpec(memory_space=pltpu.HBM)


def params(mib):
    return pltpu.CompilerParams(vmem_limit_bytes=mib * MIB)


def cost(flops, data):
    return pl.CostEstimate(flops=flops, bytes_accessed=data, transcendentals=0)


def shape(dims, dtype):
    return jax.ShapeDtypeStruct(dims, dtype)


def mm(a, b):
    return jnp.dot(a, b, preferred_element_type=f32)


def mm_nt(a, b):
    return lax.dot_general(a, b, (((1,), (1,)), ((), ())), preferred_element_type=f32)


def mm_tn(a, b):
    return lax.dot_general(a, b, (((0,), (0,)), ((), ())), preferred_element_type=f32)


def route_kernel(owner_ref, row_ref, look_ref, request_ref, pos_ref, clash_ref):
    owner = owner_ref[...]
    row = row_ref[...] + 1
    member = lax.broadcasted_iota(i32, (N_DP, UNIQ), 0) == owner
    ones = member.astype(f32).astype(bf16)
    upper = lax.broadcasted_iota(i32, (UNIQ, UNIQ), 0) < lax.broadcasted_iota(
        i32, (UNIQ, UNIQ), 1
    )
    before = mm(ones, upper.astype(f32).astype(bf16))
    within = jnp.sum(jnp.where(member, before, 0.0), axis=0, keepdims=True).astype(i32)
    pos_ref[...] = owner * CAP + within
    place = (lax.broadcasted_iota(i32, (CAP, UNIQ), 0) == within).astype(f32).astype(bf16)
    high = jnp.where(member, (row >> 6).astype(f32), 0.0).astype(bf16)
    low = jnp.where(member, (row & 63).astype(f32), 0.0).astype(bf16)
    total = mm_nt(high, place) * 64.0 + mm_nt(low, place)
    request_ref[...] = total.astype(i32) - 1
    look = look_ref[...]
    rows = LOOK // 128
    lane = lax.broadcasted_iota(i32, (rows, 128), 1) & (GROUP - 1)
    clash = jnp.zeros((rows, 128), f32)
    for shift in range(1, GROUP):
        same = (look == pltpu.roll(look, shift, 1)) & (lane >= shift)
        clash = jnp.maximum(clash, same.astype(f32))
    group = lax.broadcasted_iota(i32, (128, 128 // GROUP), 0) // GROUP
    gather = group == lax.broadcasted_iota(i32, (128, 128 // GROUP), 1)
    clash_ref[...] = mm(clash.astype(bf16), gather.astype(f32).astype(bf16)).astype(i32)


def route(owner, row, look):
    return pl.pallas_call(
        route_kernel,
        out_shape=(
            shape((N_DP, CAP), i32),
            shape((1, UNIQ), i32),
            shape((LOOK // 128, 128 // GROUP), i32),
        ),
        in_specs=[VMEM] * 3,
        out_specs=[VMEM] * 3,
        compiler_params=params(16),
        name="route",
    )(owner, row, look)


def found_kernel(asked_ref, table_ref, found_ref, rows_ref):
    def body(k, _):
        for j in range(16):
            at = k * 16 + j
            rows_ref[pl.ds(at, 1), :] = table_ref[pl.ds(asked_ref[at], 1), :]
        return 0

    lax.fori_loop(0, SLOTS // 16, body, 0)
    found_ref[...] = rows_ref[...].astype(bf16)


def found_rows(asked, table):
    return pl.pallas_call(
        found_kernel,
        out_shape=shape((SLOTS, EMB), bf16),
        in_specs=[SMEM, VMEM],
        out_specs=VMEM,
        scratch_shapes=[pltpu.VMEM((SLOTS, EMB), f32)],
        compiler_params=params(16),
        name="found",
    )(asked, table)


def counts_kernel(first_ref, look_ref, bag_ref, counts_ref, acc_ref):
    acc_ref[...] = jnp.zeros_like(acc_ref)

    def body(k, _):
        start, in_bag = bags_of(first_ref, bag_ref, k)
        slots = look_ref[pl.ds(k, 1), :] - HOT
        in_slot = (lax.broadcasted_iota(i32, (UNIQ, BLOCK), 0) == slots).astype(f32).astype(bf16)
        acc_ref[pl.ds(start, WINDOW), :] += mm_nt(in_bag, in_slot)
        return 0

    lax.fori_loop(0, BLOCKS, body, 0)
    counts_ref[...] = acc_ref[0:BAGS, :].astype(bf16)


def slot_counts(first, look, bags):
    return pl.pallas_call(
        counts_kernel,
        out_shape=shape((BAGS, UNIQ), bf16),
        in_specs=[SMEM, VMEM, VMEM],
        out_specs=VMEM,
        scratch_shapes=[pltpu.VMEM((PADDED, UNIQ), f32)],
        compiler_params=params(18),
        cost_estimate=cost(5 * 10**9, 8 * MIB),
        name="counts",
    )(first, look, bags)


def bags_of(first_ref, bag_ref, k):
    start = pl.multiple_of((first_ref[k] // 16) * 16, 16)
    bags = bag_ref[pl.ds(k, 1), :] - start
    in_bag = lax.broadcasted_iota(i32, (WINDOW, BLOCK), 0) == bags
    return start, in_bag.astype(f32).astype(bf16)


CHUNKS = 8


def pool_kernel(
    first_ref, look_ref, bag_ref, slab_ref, pooled_ref, slab_vmem, table_ref, rows_ref, acc_ref, sems
):
    height = HOT // CHUNKS

    def copy(c):
        rows = pl.ds(c * height, height)
        return pltpu.make_async_copy(slab_ref.at[rows], slab_vmem.at[rows], sems.at[c])

    for c in range(CHUNKS):
        copy(c).start()
    acc_ref[...] = jnp.zeros_like(acc_ref)
    table_ref[HOT:, :] = jnp.zeros((GROUP, EMB), f32)
    for c in range(CHUNKS):
        copy(c).wait()

        def widen(q, _, c=c):
            rows = pl.ds(pl.multiple_of(c * height + q * 512, 512), 512)
            table_ref[rows, :] = slab_vmem[rows, :].astype(f32)
            return 0

        lax.fori_loop(0, height // 512, widen, 0)

    def gather(q, _):
        for j in range(32):
            at = q * 32 + j
            rows_ref[pl.ds(at, 1), :] = table_ref[pl.ds(look_ref[at], 1), :]
        return 0

    lax.fori_loop(0, LOOK // 32, gather, 0)

    def batch(q, _):
        parts = []
        for j in range(BATCH):
            k = q * BATCH + j
            start, in_bag = bags_of(first_ref, bag_ref, k)
            rows = rows_ref[pl.ds(pl.multiple_of(k * BLOCK, BLOCK), BLOCK), :].astype(bf16)
            parts.append((start, mm(in_bag, rows)))
        for start, part in parts:
            acc_ref[pl.ds(start, WINDOW), :] += part
        return 0

    lax.fori_loop(0, BLOCKS // BATCH, batch, 0)
    pooled_ref[...] = acc_ref[0:BAGS, :]


def pool_hot(first, look, bags, slab):
    return pl.pallas_call(
        pool_kernel,
        out_shape=shape((BAGS, EMB), f32),
        in_specs=[SMEM, SMEM, VMEM, HBM],
        out_specs=VMEM,
        scratch_shapes=[
            pltpu.VMEM((HOT, EMB), bf16),
            pltpu.VMEM((HOT + GROUP, EMB), f32),
            pltpu.VMEM((LOOK, EMB), f32),
            pltpu.VMEM((PADDED, EMB), f32),
            pltpu.SemaphoreType.DMA((CHUNKS,)),
        ],
        compiler_params=params(33),
        cost_estimate=cost(10**9, 40 * MIB),
        name="pool",
    )(first, look, bags, slab)


def layer_kernel(
    pos_ref,
    pooled_ref,
    counts_ref,
    returned_ref,
    target_ref,
    weight_ref,
    out_weight_ref,
    bag_grad_ref,
    outgoing_ref,
    factors_ref,
    out_grad_ref,
    wide_ref,
    slots_ref,
):
    wide_ref[...] = returned_ref[...].astype(f32)

    def fetch(k, _):
        for j in range(16):
            at = k * 16 + j
            slots_ref[pl.ds(at, 1), :] = wide_ref[pl.ds(pos_ref[at], 1), :]
        return 0

    lax.fori_loop(0, UNIQ // 16, fetch, 0)
    counts = counts_ref[...]
    bag_grad_ref[...] = pooled_ref[...] + mm(counts, slots_ref[...].astype(bf16))
    pooled_in = jnp.concatenate(
        [bag_grad_ref[pl.ds(f, B_DEV, stride=FEAT), :] for f in range(FEAT)], axis=1
    ).astype(bf16)
    weight = weight_ref[...]
    out_weight = out_weight_ref[...]
    preact = mm(pooled_in, weight)
    gate = jax.nn.sigmoid(preact)
    act = (preact * gate).astype(bf16).astype(f32)
    logits = jnp.sum(act * out_weight, axis=1, keepdims=True)
    logit_grad = jax.nn.sigmoid(logits) - target_ref[...]
    out_grad_ref[...] = jnp.sum(act * logit_grad, axis=0, keepdims=True)
    act_grad = (logit_grad * out_weight * gate * (1.0 + preact * (1.0 - gate))).astype(bf16)
    factors_ref[0] = pooled_in
    factors_ref[1] = act_grad
    input_grad = mm_nt(act_grad, weight)
    for f in range(FEAT):
        bag_grad_ref[pl.ds(f, B_DEV, stride=FEAT), :] = input_grad[:, f * EMB : (f + 1) * EMB]

    grads = bag_grad_ref[...]
    high = grads.astype(bf16)
    low = (grads - high.astype(f32)).astype(bf16)
    both = mm_tn(counts, jnp.concatenate([high, low], axis=1))
    slots_ref[...] = both[:, :EMB] + both[:, EMB:]
    wide_ref[...] = jnp.zeros_like(wide_ref)

    def put(k, _):
        for j in range(16):
            at = k * 16 + j
            wide_ref[pl.ds(pos_ref[at], 1), :] = slots_ref[pl.ds(at, 1), :]
        return 0

    lax.fori_loop(0, UNIQ // 16, put, 0)
    outgoing_ref[...] = wide_ref[...].astype(bf16)


def layer(pos, pooled, counts, returned, target, weight, out_weight):
    return pl.pallas_call(
        layer_kernel,
        out_shape=(
            shape((BAGS, EMB), f32),
            shape((SLOTS, EMB), bf16),
            shape((2, B_DEV, HID), bf16),
            shape((1, HID), f32),
        ),
        in_specs=[SMEM] + [VMEM] * 6,
        out_specs=[VMEM] * 4,
        scratch_shapes=[pltpu.VMEM((SLOTS, EMB), f32), pltpu.VMEM((UNIQ, EMB), f32)],
        compiler_params=params(30),
        cost_estimate=cost(4 * 10**9, 20 * MIB),
        name="layer",
    )(pos, pooled, counts, returned, target, weight, out_weight)


def hidden_kernel(mine_ref, one_ref, two_ref, hidden_ref):
    at = lax.broadcasted_iota(i32, (1, HID // 2), 1) ^ mine_ref[0]
    x_high, y_high = (at >> 8) & 1, (at >> 6) & 1
    x = 2 * x_high + (x_high ^ ((at >> 7) & 1))
    y = 2 * y_high + (y_high ^ ((at >> 5) & 1))
    source = ((((at >> 2) & 7) * 4 + x) * 2 + (at >> 9)) * 16 + y * 4 + (at & 3)
    order = (lax.broadcasted_iota(i32, (HID, HID // 2), 0) == source).astype(f32).astype(bf16)
    total = mm_tn(mm(one_ref[0], order).astype(bf16), one_ref[1])
    hidden_ref[...] = total + mm_tn(mm(two_ref[0], order).astype(bf16), two_ref[1])


def hidden_half(mine, one, two):
    return pl.pallas_call(
        hidden_kernel,
        out_shape=shape((HID // 2, HID), f32),
        in_specs=[SMEM, VMEM, VMEM],
        out_specs=VMEM,
        compiler_params=params(24),
        cost_estimate=cost(4 * 10**9, 4 * MIB),
        name="hidden_half",
    )(mine, one, two)


def scatter_kernel(
    look_ref, clash_ref, clashes_ref, first_ref, mine_ref, bag_ref, grad_ref, keep_ref, send_ref, acc_ref, halves_ref, rows_ref
):
    grads = grad_ref[...]
    high, low = split(grads)
    halves_ref[0:BAGS, 0:EMB] = high
    halves_ref[0:BAGS, EMB:] = low
    halves_ref[BAGS:, :] = jnp.zeros((PADDED - BAGS, 2 * EMB), bf16)

    def stage(q, _):
        for j in range(BATCH):
            k = q * BATCH + j
            start, in_bag = bags_of(first_ref, bag_ref, k)
            both = mm_tn(in_bag, halves_ref[pl.ds(start, WINDOW), :])
            rows_ref[pl.ds(pl.multiple_of(k * BLOCK, BLOCK), BLOCK), :] = (
                both[:, :EMB] + both[:, EMB:]
            )
        acc_rows = HOT // (BLOCKS // BATCH)
        for j in range(acc_rows // 512):
            acc_ref[pl.ds(pl.multiple_of(q * acc_rows + j * 512, 512), 512), :] = jnp.zeros(
                (512, EMB), f32
            )
        return 0

    lax.fori_loop(0, BLOCKS // BATCH, stage, 0)

    def distinct(at):
        rows = [look_ref[at + m] for m in range(GROUP)]
        sums = [
            acc_ref[pl.ds(rows[m], 1), :] + rows_ref[pl.ds(at + m, 1), :] for m in range(GROUP)
        ]
        for m in range(GROUP):
            acc_ref[pl.ds(rows[m], 1), :] = sums[m]

    def block(k, _):
        @pl.when(clashes_ref[k] == 0)
        def _():
            def pair(q, _):
                distinct(k * BLOCK + q * 2 * GROUP)
                distinct(k * BLOCK + q * 2 * GROUP + GROUP)
                return 0

            lax.fori_loop(0, BLOCK // GROUP // 2, pair, 0)

        @pl.when(clashes_ref[k] != 0)
        def _():
            def group(q, _):
                at = k * BLOCK + q * GROUP
                clash = clash_ref[k * (BLOCK // GROUP) + q]

                @pl.when(clash == 0)
                def _():
                    distinct(at)

                @pl.when(clash != 0)
                def _():
                    for m in range(GROUP):
                        acc_ref[pl.ds(look_ref[at + m], 1), :] += rows_ref[pl.ds(at + m, 1), :]

                return 0

            lax.fori_loop(0, BLOCK // GROUP, group, 0)

        return 0

    lax.fori_loop(0, BLOCKS, block, 0)

    core, bits = mine_ref[1], mine_ref[2]
    for s in range(4):

        def gather(k, _, s=s):
            bit = [(bits >> (3 - axis)) & 1 for axis in range(4)]
            for j, axis in enumerate(ORDERS[s]):
                bit[axis] = bit[axis] ^ ((k >> (3 - j)) & 1)
            x = 2 * bit[0] + (bit[0] ^ bit[1])
            y = 2 * bit[2] + (bit[2] ^ bit[3])
            base = x * 1024 + y * 128 + 32 * s
            own = pl.multiple_of(base + 512 * core, 32)
            other = pl.multiple_of(base + 512 * (1 - core), 32)
            for z in range(8):
                keep_ref[s, k, z] = acc_ref[pl.ds(own + z * 4096, 32), :]
                send_ref[s, k, z] = acc_ref[pl.ds(other + z * 4096, 32), :].astype(bf16)
            return 0

        lax.fori_loop(0, 16, gather, 0)


def scatter_hot(look, clash, clashes, first, mine, bags, grads):
    return pl.pallas_call(
        scatter_kernel,
        out_shape=(shape((4, 16, 8, 32, EMB), f32), shape((4, 16, 8, 32, EMB), bf16)),
        in_specs=[SMEM] * 5 + [VMEM] * 2,
        out_specs=[VMEM] * 2,
        scratch_shapes=[
            pltpu.VMEM((HOT + GROUP, EMB), f32),
            pltpu.VMEM((PADDED, 2 * EMB), bf16),
            pltpu.VMEM((LOOK, EMB), f32),
        ],
        compiler_params=params(40),
        cost_estimate=cost(10**9, 80 * MIB),
        name="scatter",
    )(look, clash, clashes, first, mine, bags, grads)


def split(values):
    high = values.astype(bf16)
    return high, (values - high.astype(f32)).astype(bf16)


def hot_parts(count):
    return 2 if count <= 2 else 1


def put_hot(send_ref, count, at, total):
    if hot_parts(count) == 2:
        high, low = split(total)
        send_ref[count * 256 + at * 256 : count * 256 + at * 256 + 256, :] = low
    else:
        high = total.astype(bf16)
    send_ref[at * 256 : at * 256 + 256, :] = high


def get_hot(recv_ref, count, at):
    high = recv_ref[at * 256 : at * 256 + 256, :].astype(f32)
    if hot_parts(count) == 2:
        base = count * 256 + at * 256
        high = high + recv_ref[base : base + 256, :].astype(f32)
    return high


def hidden_base(count):
    return count * 256 * hot_parts(count)


def put_hidden(send_ref, count, at, total):
    high, low = split(total)
    base = hidden_base(count) + at * 128
    for part, values in enumerate((high, low)):
        for half in range(2):
            row = base + part * 64 + half * 32
            send_ref[row : row + 32, :] = values[:, half * 128 : half * 128 + 128]


def get_hidden(recv_ref, count, at):
    base = hidden_base(count) + at * 128
    pieces = [recv_ref[base + 32 * q : base + 32 * q + 32, :].astype(f32) for q in range(4)]
    return jnp.concatenate([pieces[0] + pieces[2], pieces[1] + pieces[3]], axis=1)


def out_base(count):
    return hidden_base(count) + count * 128


def put_out(send_ref, count, total):
    high = total.astype(bf16).astype(f32)
    send_ref[out_base(count) : out_base(count) + 16, :] = jnp.concatenate(
        [high, total - high], axis=0
    ).astype(bf16)


def get_out(recv_ref, count):
    wide = recv_ref[out_base(count) : out_base(count) + 16, :].astype(f32)
    return wide[0:8] + wide[8:16]


def rounded_out(total):
    high = total.astype(bf16).astype(f32)
    return high + (total - high).astype(bf16).astype(f32)


def place_of(s, step, k):
    left = sorted(ORDERS[s][step:])
    bit = len(left) - 1 - left.index(ORDERS[s][step])
    rest = ((k >> (bit + 1)) << bit) | (k & ((1 << bit) - 1))
    return (k >> bit) & 1, rest


def send_shapes(count):
    return tuple(
        shape((out_base(count) + (16 if s == 0 else 0), EMB), bf16) for s in range(4)
    ) + (shape((8, EMB), f32),)


def keep_shapes(count):
    return tuple(shape((count, 8, 32, EMB), f32) for s in range(4)) + tuple(
        shape((count, 32, 256), f32) for s in range(4)
    )


def first_send_kernel(keep_ref, recv_ref, hidden_ref, out_ref, out_recv_ref, *outs):
    for s in range(4):

        def hot(k, _, s=s):
            total = keep_ref[s, k + 8].reshape(256, EMB) + recv_ref[s, k + 8].astype(f32).reshape(
                256, EMB
            )
            outs[s][pl.ds(pl.multiple_of(k * 256, 256), 256), :] = total.astype(bf16)
            return 0

        lax.fori_loop(0, 8, hot, 0)
        for k in range(16):
            flag, rest = place_of(s, 0, k)
            if flag:
                put_hidden(
                    outs[s], 8, rest, hidden_ref[32 * k : 32 * k + 32, 256 * s : 256 * s + 256]
                )
    total = out_ref[...] + out_recv_ref[...]
    outs[4][...] = total
    put_out(outs[0], 8, total)


def first_send(keep, recv, hidden, out, out_recv):
    return pl.pallas_call(
        first_send_kernel,
        out_shape=send_shapes(8),
        in_specs=[VMEM] * 5,
        out_specs=[VMEM] * 5,
        compiler_params=params(24),
        cost_estimate=cost(10**6, 12 * MIB),
        name="first_send",
    )(keep, recv, hidden, out, out_recv)


def first_keep_kernel(keep_ref, recv_ref, hidden_ref, *outs):
    for s in range(4):

        def hot(k, _, s=s):
            outs[s][k] = keep_ref[s, k] + recv_ref[s, k].astype(f32)
            return 0

        lax.fori_loop(0, 8, hot, 0)
        for k in range(16):
            flag, rest = place_of(s, 0, k)
            if not flag:
                outs[4 + s][rest] = hidden_ref[32 * k : 32 * k + 32, 256 * s : 256 * s + 256]


def first_keep(keep, recv, hidden):
    return pl.pallas_call(
        first_keep_kernel,
        out_shape=keep_shapes(8),
        in_specs=[VMEM] * 3,
        out_specs=[VMEM] * 8,
        compiler_params=params(24),
        cost_estimate=cost(10**6, 12 * MIB),
        name="first_keep",
    )(keep, recv, hidden)


def next_kernel(step, *refs):
    count = 16 >> step
    recvs, out_ref, hots, hiddens = refs[0:4], refs[4], refs[5:9], refs[9:13]
    sends, out_new_ref, hot_outs, hidden_outs = refs[13:17], refs[17], refs[18:22], refs[22:26]
    for s in range(4):
        for k in range(count):
            total = hots[s][k].reshape(256, EMB) + get_hot(recvs[s], count, k)
            if k >= count // 2:
                put_hot(sends[s], count // 2, k - count // 2, total)
            else:
                hot_outs[s][k] = total.reshape(8, 32, EMB)
            flag, rest = place_of(s, step, k)
            hidden = hiddens[s][k] + get_hidden(recvs[s], count, k)
            if flag:
                put_hidden(sends[s], count // 2, rest, hidden)
            else:
                hidden_outs[s][rest] = hidden
    total = rounded_out(out_ref[...]) + get_out(recvs[0], count)
    out_new_ref[...] = total
    put_out(sends[0], count // 2, total)


def next_step(step, sends, keeps):
    count = 16 >> step
    values = pl.pallas_call(
        lambda *refs: next_kernel(step, *refs),
        out_shape=send_shapes(count // 2) + keep_shapes(count // 2),
        in_specs=[VMEM] * 13,
        out_specs=[VMEM] * 13,
        compiler_params=params(24),
        cost_estimate=cost(10**6, count * 2 * MIB),
        name="step_" + str(step + 1),
    )(*sends, *keeps)
    return values[:5], values[5:]


Z_ROWS = 336


def last_kernel(*refs):
    recvs, sum_ref, hots, hiddens, out_ref, pieces_ref = (
        refs[0:4], refs[4], refs[5:9], refs[9:13], refs[13], refs[14],
    )
    for s in range(4):
        total = hots[s][0].reshape(256, EMB) + get_hot(recvs[s], 1, 0)
        hidden = hiddens[s][0] + get_hidden(recvs[s], 1, 0)
        high, low = split(total)
        for z in range(8):
            out_ref[z, 32 * s : 32 * s + 32, :] = high[32 * z : 32 * z + 32]
            out_ref[z, 128 + 32 * s : 160 + 32 * s, :] = low[32 * z : 32 * z + 32]
            for half in range(2):
                row = (2 * s + half) * 4
                pieces_ref[z, row : row + 4, :] = hidden[
                    4 * z : 4 * z + 4, half * 128 : half * 128 + 128
                ]
    total = rounded_out(sum_ref[...]) + get_out(recvs[0], 1)
    high = total.astype(bf16).astype(f32)
    both = jnp.concatenate([high, total - high], axis=0).astype(bf16)
    for z in range(8):
        high, low = split(pieces_ref[z])
        out_ref[z, 256:288, :] = high
        out_ref[z, 288:320, :] = low
        out_ref[z, 320:336, :] = both


def last_step(sends, keeps):
    return pl.pallas_call(
        last_kernel,
        out_shape=shape((8, Z_ROWS, EMB), bf16),
        in_specs=[VMEM] * 13,
        out_specs=VMEM,
        scratch_shapes=[pltpu.VMEM((8, 32, EMB), f32)],
        compiler_params=params(16),
        cost_estimate=cost(10**6, 2 * MIB),
        name="step_5",
    )(*sends, *keeps)


def row_update(param, accum_row, grad):
    turned = grad.T
    accum_new = accum_row + jnp.sum(turned * turned, axis=0, keepdims=True) * (1.0 / EMB)
    return param - (learn_rate * turned / jnp.sqrt(accum_new)).T, accum_new


def update_kernel(
    recv_ref, slab_ref, accum_ref, weight_ref, hid_accum_ref, new_ref, accum_new_ref, weight_new_ref, hid_new_ref, out_ref
):
    total = jnp.sum(recv_ref[...].astype(f32), axis=0)
    new_ref[...], accum_new_ref[...] = row_update(
        slab_ref[...].astype(f32), accum_ref[...], total[0:128] + total[128:256]
    )
    hidden = total[256:288] + total[288:320]
    for part in range(8):
        columns = slice(part * 128, part * 128 + 128)
        grad = hidden[part * 4 : part * 4 + 4]
        accum_new = hid_accum_ref[:, columns] + grad * grad
        hid_new_ref[:, columns] = accum_new
        weight_new_ref[:, columns] = weight_ref[:, columns] - learn_rate * grad / jnp.sqrt(accum_new)
    out_ref[...] = total[320:328] + total[328:336]


def update_owned(recv, slab, accum, weight, hid_accum):
    return pl.pallas_call(
        update_kernel,
        out_shape=(
            shape((128, EMB), f32),
            shape((1, 128), f32),
            shape((4, HID), f32),
            shape((4, HID), f32),
            shape((8, EMB), f32),
        ),
        in_specs=[VMEM] * 5,
        out_specs=[VMEM] * 5,
        compiler_params=params(16),
        name="update",
    )(recv, slab, accum, weight, hid_accum)


def cold_grad_kernel(asked_ref, incoming_ref, a_ref, b_ref):
    asked = asked_ref[...]
    incoming = incoming_ref[...]
    for part in range(8):
        rows = lax.broadcasted_iota(i32, (256, SLOTS), 0) + part * 256
        total = mm((rows == asked).astype(f32).astype(bf16), incoming).astype(bf16)
        if part < 4:
            a_ref[part * 256 : part * 256 + 256, :] = total
        else:
            b_ref[part * 256 - 1024 : part * 256 - 768, :] = total


def cold_grads(asked, incoming):
    return pl.pallas_call(
        cold_grad_kernel,
        out_shape=(shape((1024, EMB), bf16),) * 2,
        in_specs=[VMEM] * 2,
        out_specs=[VMEM] * 2,
        compiler_params=params(24),
        cost_estimate=cost(2 * 10**9, 4 * MIB),
        name="cold_grads",
    )(asked, incoming)


def pair_kernel(a, b, c, d, e_ref, f_ref):
    e_ref[...] = (a[...].astype(f32) + b[...].astype(f32)).astype(bf16)
    f_ref[...] = (c[...].astype(f32) + d[...].astype(f32)).astype(bf16)


def pair_sums(a, b, c, d):
    return pl.pallas_call(
        pair_kernel,
        out_shape=(shape((1024, EMB), bf16),) * 2,
        in_specs=[VMEM] * 4,
        out_specs=[VMEM] * 2,
        compiler_params=params(16),
        name="pair_sums",
    )(a, b, c, d)


def cold_update_kernel(a, b, c, d, table_ref, accum_ref, new_ref, accum_new_ref):
    for block in range(16):
        one, two = (a, b) if block < 8 else (c, d)
        at = slice((block % 8) * 128, (block % 8) * 128 + 128)
        rows = slice(block * 128, block * 128 + 128)
        grad = one[at, :].astype(f32) + two[at, :].astype(f32)
        new_ref[rows, :], accum_new_ref[block : block + 1, :] = row_update(
            table_ref[rows, :], accum_ref[block : block + 1, :], grad
        )


def update_cold(a, b, c, d, table, accum):
    return pl.pallas_call(
        cold_update_kernel,
        out_shape=(shape((R_OWN, EMB), f32), shape((R_OWN // 128, 128), f32)),
        in_specs=[VMEM] * 6,
        out_specs=[VMEM] * 2,
        compiler_params=params(16),
        name="cold_update",
    )(a, b, c, d, table, accum)


def dp_index(z, x, core):
    return (z * 4 + x) * 2 + core


def over_core(value):
    pairs = [
        (dp_index(z, x, core), dp_index(z, x, 1 - core))
        for z in range(8)
        for x in range(4)
        for core in range(2)
    ]
    return lax.ppermute(value, "dp", pairs)


def over_axis(value, axis):
    swap = (lambda i: 3 - i) if axis in (0, 2) else (lambda i: i ^ 1)
    if axis >= 2:
        return lax.ppermute(value, "rep", [(y, swap(y)) for y in range(4)])
    pairs = [
        (dp_index(z, x, core), dp_index(z, swap(x), core))
        for z in range(8)
        for x in range(4)
        for core in range(2)
    ]
    return lax.ppermute(value, "dp", pairs)


def over_z(value):
    groups = [[dp_index(z, x, core) for z in range(8)] for x in range(4) for core in range(2)]
    return lax.all_to_all(
        value, "dp", split_axis=0, concat_axis=0, tiled=True, axis_index_groups=groups
    )


def on_device(
    hot_slab,
    hot_accum,
    cold_table,
    cold_accum,
    touched_owner,
    touched_row,
    lookup_index,
    bag_id,
    labels,
    w_hidden,
    hidden_accum,
    w_out,
    out_accum,
):
    dp = lax.axis_index("dp")
    y = lax.axis_index("rep")
    core, x = dp & 1, (dp >> 1) & 3
    position = dp * 4 + y
    bits = ((x ^ (x >> 1)) << 2) | (y ^ (y >> 1))
    mine = jnp.stack([(core << 9) | (bits << 5), core, bits]).astype(i32)

    rows = LOOK // 128
    look = lookup_index.reshape(rows, 128)
    spare = HOT + (lax.broadcasted_iota(i32, (rows, 128), 1) & (GROUP - 1))
    look = jnp.where(look < HOT, look, spare)
    look_flat = look.reshape(LOOK)
    bag_rows = bag_id.reshape(BLOCKS, BLOCK)
    first = bag_rows[:, 0]

    requests, pos, clash = route(
        touched_owner.reshape(1, UNIQ), touched_row.reshape(1, UNIQ), look
    )
    pos_flat = pos.reshape(UNIQ)
    counts = slot_counts(first, lookup_index.reshape(BLOCKS, BLOCK), bag_rows)
    asked = lax.all_to_all(requests, "dp", split_axis=0, concat_axis=0, tiled=True)
    asked, counts = lax.optimization_barrier((asked, counts))
    found = found_rows(jnp.maximum(asked, 0).reshape(SLOTS), cold_table)
    returned = lax.all_to_all(
        found.reshape(N_DP, CAP, EMB), "dp", split_axis=0, concat_axis=0, tiled=True
    ).reshape(SLOTS, EMB)
    pooled = pool_hot(first, look_flat, bag_rows, hot_slab)
    bag_grad, outgoing, factors, out_grad = layer(
        pos_flat,
        pooled,
        counts,
        returned,
        labels.reshape(B_DEV, 1),
        w_hidden,
        w_out.reshape(1, HID),
    )
    incoming = lax.all_to_all(
        outgoing.reshape(N_DP, CAP, EMB), "dp", split_axis=0, concat_axis=0, tiled=True
    ).reshape(SLOTS, EMB)
    other_factors = over_core(factors)
    out_grad = out_grad.reshape(8, EMB)
    out_recv = over_core(out_grad)
    clashes = jnp.max(clash.reshape(BLOCKS, BLOCK // GROUP), axis=1)
    keep, send = scatter_hot(
        look_flat, clash.reshape(LOOK // GROUP), clashes, first, mine, bag_rows, bag_grad
    )
    send, incoming = lax.optimization_barrier((send, incoming))
    recv = over_core(send)
    hidden = hidden_half(mine, factors, other_factors)
    cold_a, cold_b = cold_grads(asked.reshape(1, SLOTS), incoming)
    recv_a, recv_b = over_axis(cold_a, 3), over_axis(cold_b, 2)
    sends = first_send(keep, recv, hidden, out_grad, out_recv)
    recv_a, recv_b, *sends = lax.optimization_barrier((recv_a, recv_b, *sends))
    keeps = first_keep(keep, recv, hidden)
    for step in range(4):
        travelled = [over_axis(sends[s], ORDERS[s][step]) for s in range(4)] + [sends[4]]
        if step < 3:
            sends, keeps = next_step(step + 1, travelled, keeps)
    pair_a, pair_b = pair_sums(cold_a, recv_a, cold_b, recv_b)
    parts, pair_a, pair_b = lax.optimization_barrier((last_step(travelled, keeps), pair_a, pair_b))
    recv_a, recv_b = over_axis(pair_a, 2), over_axis(pair_b, 3)
    parts = over_z(parts)
    cold_new, cold_accum_new = update_cold(
        pair_a, recv_a, pair_b, recv_b, cold_table, cold_accum.reshape(R_OWN // 128, 128)
    )

    own_slab = lax.dynamic_slice_in_dim(hot_slab, position * 128, 128, 0)
    own_hidden = lax.dynamic_slice_in_dim(w_hidden, position * 4, 4, 0).astype(f32)
    own_out = lax.dynamic_slice_in_dim(w_out, position * 4, 4, 0)
    hot_new, hot_accum_new, hidden_new, hidden_accum_new, out_total = update_owned(
        parts, own_slab, hot_accum.reshape(1, 128), own_hidden, hidden_accum
    )
    out_part = lax.dynamic_slice_in_dim(out_total.reshape(HID), position * 4, 4, 0)
    out_accum_new = out_accum + out_part * out_part
    out_new = own_out - learn_rate * out_part / jnp.sqrt(out_accum_new)
    return (
        hot_new,
        hot_accum_new.reshape(128),
        cold_new,
        cold_accum_new.reshape(R_OWN),
        hidden_new,
        hidden_accum_new,
        out_new,
        out_accum_new,
    )


def solution(mesh):
    both = ("dp", "rep")
    in_specs = (
        P(),
        P(both),
        P("dp", None),
        P("dp"),
        P(both, None),
        P(both),
        P(both),
        P(both, None),
        P(both),
        P(),
        P(both, None),
        P(),
        P(both),
    )
    out_specs = (
        P(both, None),
        P(both),
        P("dp", None),
        P("dp"),
        P(both, None),
        P(both, None),
        P(both),
        P(both),
    )
    return jax.shard_map(
        on_device, mesh=mesh, in_specs=in_specs, out_specs=out_specs, check_vma=False
    )
```

```python
import jax
import jax.numpy as jnp
from jax import lax
from jax.experimental import pallas as pl
from jax.experimental.pallas import tpu as pltpu
from jax.sharding import PartitionSpec as P

learn_rate = 0.05
bf16 = jnp.bfloat16
f32 = jnp.float32
i32 = jnp.int32

EMB = 128
HOT = 32768
FEAT = 8
HID = 1024
B_DEV = 256
BAGS = 2048
LOOK = 8192
UNIQ = 1024
CAP = 48
R_OWN = 2048
N_DP = 64
SLOTS = N_DP * CAP
GROUP = 16
BLOCK = 256
WINDOW = BLOCK + 16
BLOCKS = LOOK // BLOCK
BATCH = 4
FLAGS = 128
ANY = FLAGS - 1
LAST_START = BAGS - WINDOW
MIB = 1 << 20

ORDERS = ((3, 2, 1, 0), (2, 3, 0, 1), (1, 0, 3, 2), (0, 1, 2, 3))

SMEM = pl.BlockSpec(memory_space=pltpu.SMEM)
VMEM = pl.BlockSpec(memory_space=pltpu.VMEM)
HBM = pl.BlockSpec(memory_space=pltpu.HBM)


def params(mib):
    return pltpu.CompilerParams(vmem_limit_bytes=mib * MIB)


def cost(flops, data):
    return pl.CostEstimate(flops=flops, bytes_accessed=data, transcendentals=0)


def shape(dims, dtype):
    return jax.ShapeDtypeStruct(dims, dtype)


def mm(a, b):
    return jnp.dot(a, b, preferred_element_type=f32)


def mm_nt(a, b):
    return lax.dot_general(a, b, (((1,), (1,)), ((), ())), preferred_element_type=f32)


def mm_tn(a, b):
    return lax.dot_general(a, b, (((0,), (0,)), ((), ())), preferred_element_type=f32)


def route_kernel(owner_ref, row_ref, request_ref, pos_ref):
    owner = owner_ref[...]
    row = row_ref[...]
    member = lax.broadcasted_iota(i32, (N_DP, UNIQ), 0) == owner
    ones = member.astype(f32).astype(bf16)
    upper = lax.broadcasted_iota(i32, (UNIQ, UNIQ), 0) < lax.broadcasted_iota(
        i32, (UNIQ, UNIQ), 1
    )
    before = mm(ones, upper.astype(f32).astype(bf16))
    within = jnp.sum(jnp.where(member, before, 0.0), axis=0, keepdims=True).astype(i32)
    pos_ref[...] = owner * CAP + within
    place = (lax.broadcasted_iota(i32, (CAP, UNIQ), 0) == within).astype(f32).astype(bf16)
    high = jnp.where(member, (row >> 6).astype(f32), 0.0).astype(bf16)
    low = jnp.where(member, (row & 63).astype(f32), 0.0).astype(bf16)
    total = mm_nt(high, place) * 64.0 + mm_nt(low, place)
    request_ref[...] = total.astype(i32)


def route(owner, row):
    return pl.pallas_call(
        route_kernel,
        out_shape=(shape((N_DP, CAP), i32), shape((1, UNIQ), i32)),
        in_specs=[VMEM] * 2,
        out_specs=[VMEM] * 2,
        compiler_params=params(16),
        name="route",
    )(owner, row)


def clash_kernel(look_ref, hot_ref, clash_ref):
    rows = LOOK // 128
    lane = lax.broadcasted_iota(i32, (rows, 128), 1) & (GROUP - 1)
    look = look_ref[...]
    look = jnp.where(look < HOT, look, HOT + lane)
    hot_ref[...] = look
    clash = jnp.zeros((rows, 128), f32)
    for shift in range(1, GROUP):
        same = (look == pltpu.roll(look, shift, 1)) & (lane >= shift)
        clash = jnp.maximum(clash, same.astype(f32))
    group = lax.broadcasted_iota(i32, (128, FLAGS), 0) // GROUP
    column = lax.broadcasted_iota(i32, (128, FLAGS), 1)
    gather = (group == column) | (column == ANY)
    clash_ref[...] = mm(clash.astype(bf16), gather.astype(f32).astype(bf16)).astype(i32)


def clashes(look):
    return pl.pallas_call(
        clash_kernel,
        out_shape=(shape((LOOK // 128, 128), i32), shape((LOOK // 128, FLAGS), i32)),
        in_specs=[VMEM],
        out_specs=[VMEM] * 2,
        compiler_params=params(16),
        name="clashes",
    )(look)


def found_kernel(asked_ref, table_ref, found_ref, rows_ref):
    def body(owner, _):
        for j in range(CAP):
            rows_ref[pl.ds(owner * CAP + j, 1), :] = table_ref[pl.ds(asked_ref[owner, j], 1), :]
        return 0

    lax.fori_loop(0, N_DP, body, 0)
    found_ref[...] = rows_ref[...].astype(bf16)


def found_rows(asked, table):
    return pl.pallas_call(
        found_kernel,
        out_shape=shape((SLOTS, EMB), bf16),
        in_specs=[SMEM, VMEM],
        out_specs=VMEM,
        scratch_shapes=[pltpu.VMEM((SLOTS, EMB), f32)],
        compiler_params=params(16),
        name="found",
    )(asked, table)


def one_hot(height, middle, numbers):
    place = (lax.broadcasted_iota(i32, (height, 128), 0) - middle).astype(f32).astype(bf16)
    inside = (numbers >= 0) & (numbers < height)
    named = jnp.where(inside, numbers - middle, -middle - 2).astype(f32).astype(bf16)
    return jnp.where(place == named, jnp.ones((), bf16), jnp.zeros((), bf16))


def bags_of(flat_ref, bag_ref, k):
    start = jnp.minimum((flat_ref[k * BLOCK] // 16) * 16, LAST_START)
    start = pl.multiple_of(start, 16)
    in_bag = [one_hot(WINDOW, WINDOW // 2, bag_ref[pl.ds(2 * k + j, 1), :] - start) for j in range(2)]
    return start, jnp.concatenate(in_bag, axis=1)


def count_slots(base, flat_ref, look_ref, bag_ref, acc_ref):
    acc_ref[...] = jnp.zeros_like(acc_ref)
    many = acc_ref.shape[1]

    def body(q, _):
        parts = []
        for b in range(BATCH):
            k = BATCH * q + b
            start, in_bag = bags_of(flat_ref, bag_ref, k)
            in_slot = [
                one_hot(many, many // 2, look_ref[pl.ds(2 * k + j, 1), :] - (HOT + base))
                for j in range(2)
            ]
            in_slot = jnp.concatenate(in_slot, axis=1)
            parts.append((start, mm_nt(in_bag, in_slot).astype(bf16)))
        for start, part in parts:
            acc_ref[pl.ds(start, WINDOW), :] += part
        return 0

    lax.fori_loop(0, BLOCKS // BATCH, body, 0)


def counts_out(acc_ref, counts_ref, sems):
    return [
        pltpu.make_async_copy(
            acc_ref.at[pl.ds(c * 512, 512)], counts_ref.at[pl.ds(c * 512, 512)], sems.at[c]
        )
        for c in range(4)
    ]


def counts_kernel(flat_ref, look_ref, bag_ref, counts_ref, acc_ref, sems):
    count_slots(0, flat_ref, look_ref, bag_ref, acc_ref)
    copies = counts_out(acc_ref, counts_ref, sems)
    for copy in copies:
        copy.start()
    for copy in copies:
        copy.wait()


def slot_counts(flat, look, bags):
    return pl.pallas_call(
        counts_kernel,
        out_shape=shape((BAGS, UNIQ // 2), bf16),
        in_specs=[SMEM, VMEM, VMEM],
        out_specs=HBM,
        scratch_shapes=[pltpu.VMEM((BAGS, UNIQ // 2), bf16), pltpu.SemaphoreType.DMA((4,))],
        compiler_params=params(58),
        cost_estimate=cost(5 * 10**9, 8 * MIB),
        name="counts",
    )(flat, look, bags)


CHUNKS = 8


def pool_kernel(
    flat_ref,
    look_ref,
    raw_ref,
    bag_ref,
    slab_ref,
    pooled_ref,
    counts_ref,
    slab_vmem,
    table_ref,
    rows_ref,
    counts_vmem,
    sems,
    count_sems,
):
    height = HOT // CHUNKS

    def copy(c):
        rows = pl.ds(c * height, height)
        return pltpu.make_async_copy(slab_ref.at[rows], slab_vmem.at[rows], sems.at[c])

    for c in range(CHUNKS):
        copy(c).start()
    count_slots(UNIQ // 2, flat_ref, raw_ref, bag_ref, counts_vmem)
    out_copies = counts_out(counts_vmem, counts_ref, count_sems)
    for out_copy in out_copies:
        out_copy.start()
    pooled_ref[...] = jnp.zeros_like(pooled_ref)
    table_ref[HOT:, :] = jnp.zeros((GROUP, EMB), f32)
    for c in range(CHUNKS):
        copy(c).wait()

        def widen(q, _, c=c):
            rows = pl.ds(pl.multiple_of(c * height + q * 512, 512), 512)
            table_ref[rows, :] = slab_vmem[rows, :].astype(f32)
            return 0

        lax.fori_loop(0, height // 512, widen, 0)

    def gather(q, _):
        for j in range(32):
            at = q * 32 + j
            rows_ref[pl.ds(at, 1), :] = table_ref[pl.ds(look_ref[at], 1), :]
        return 0

    lax.fori_loop(0, LOOK // 32, gather, 0)

    def batch(q, _):
        parts = []
        for j in range(BATCH):
            k = q * BATCH + j
            start, in_bag = bags_of(flat_ref, bag_ref, k)
            rows = rows_ref[pl.ds(pl.multiple_of(k * BLOCK, BLOCK), BLOCK), :].astype(bf16)
            parts.append((start, mm(in_bag, rows)))
        for start, part in parts:
            pooled_ref[pl.ds(start, WINDOW), :] += part
        return 0

    lax.fori_loop(0, BLOCKS // BATCH, batch, 0)
    for out_copy in out_copies:
        out_copy.wait()


def pool_hot(flat, look, raw, bags, slab):
    return pl.pallas_call(
        pool_kernel,
        out_shape=(shape((BAGS, EMB), f32), shape((BAGS, UNIQ // 2), bf16)),
        in_specs=[SMEM, SMEM, VMEM, VMEM, HBM],
        out_specs=[VMEM, HBM],
        scratch_shapes=[
            pltpu.VMEM((HOT, EMB), bf16),
            pltpu.VMEM((HOT + GROUP, EMB), f32),
            pltpu.VMEM((LOOK, EMB), f32),
            pltpu.VMEM((BAGS, UNIQ // 2), bf16),
            pltpu.SemaphoreType.DMA((CHUNKS,)),
            pltpu.SemaphoreType.DMA((4,)),
        ],
        compiler_params=params(58),
        cost_estimate=cost(10**9, 40 * MIB),
        name="pool",
    )(flat, look, raw, bags, slab)


def layer_kernel(
    pos_ref,
    pooled_ref,
    count_a_ref,
    count_b_ref,
    returned_ref,
    target_ref,
    weight_ref,
    out_weight_ref,
    bag_grad_ref,
    outgoing_ref,
    factors_ref,
    out_grad_ref,
    wide_ref,
    slots_ref,
    counts_vmem,
    weight_vmem,
    grads_vmem,
    factors_vmem,
    sems,
):
    half = UNIQ // 2
    counts_in = [
        pltpu.make_async_copy(ref, counts_vmem.at[:, pl.ds(c * half, half)], sems.at[4 * c])
        for c, ref in enumerate((count_a_ref, count_b_ref))
    ]
    weight_in = pltpu.make_async_copy(weight_ref, weight_vmem, sems.at[1])
    grads_out = pltpu.make_async_copy(grads_vmem, bag_grad_ref, sems.at[2])
    factors_out = pltpu.make_async_copy(factors_vmem, factors_ref, sems.at[3])
    for copy in counts_in:
        copy.start()
    weight_in.start()
    wide_ref[...] = returned_ref[...].astype(f32)

    def fetch(k, _):
        for j in range(16):
            at = k * 16 + j
            slots_ref[pl.ds(at, 1), :] = wide_ref[pl.ds(pos_ref[at], 1), :]
        return 0

    lax.fori_loop(0, UNIQ // 16, fetch, 0)
    for copy in counts_in:
        copy.wait()
    counts = counts_vmem[...]
    grads_vmem[...] = pooled_ref[...] + mm(counts, slots_ref[...].astype(bf16))
    pooled_in = jnp.concatenate(
        [grads_vmem[pl.ds(f, B_DEV, stride=FEAT), :] for f in range(FEAT)], axis=1
    ).astype(bf16)
    weight_in.wait()
    weight = weight_vmem[...]
    out_weight = out_weight_ref[...]
    preact = mm(pooled_in, weight)
    gate = jax.nn.sigmoid(preact)
    act = (preact * gate).astype(bf16).astype(f32)
    logits = jnp.sum(act * out_weight, axis=1, keepdims=True)
    diagonal = lax.broadcasted_iota(i32, (B_DEV, B_DEV), 0) == lax.broadcasted_iota(
        i32, (B_DEV, B_DEV), 1
    )
    target = jnp.sum(jnp.where(diagonal, target_ref[...], 0.0), axis=1, keepdims=True)
    logit_grad = jax.nn.sigmoid(logits) - target
    out_grad_ref[...] = jnp.sum(act * logit_grad, axis=0, keepdims=True)
    act_grad = (logit_grad * out_weight * gate * (1.0 + preact * (1.0 - gate))).astype(bf16)
    factors_vmem[0] = pooled_in
    factors_vmem[1] = act_grad
    factors_out.start()
    input_grad = mm_nt(act_grad, weight)
    for f in range(FEAT):
        grads_vmem[pl.ds(f, B_DEV, stride=FEAT), :] = input_grad[:, f * EMB : (f + 1) * EMB]

    grads_out.start()
    grads = grads_vmem[...]
    high = grads.astype(bf16)
    low = (grads - high.astype(f32)).astype(bf16)
    both = mm_tn(counts, jnp.concatenate([high, low], axis=1))
    slots_ref[...] = both[:, :EMB] + both[:, EMB:]
    wide_ref[...] = jnp.zeros_like(wide_ref)

    def put(k, _):
        for j in range(16):
            at = k * 16 + j
            wide_ref[pl.ds(pos_ref[at], 1), :] = slots_ref[pl.ds(at, 1), :]
        return 0

    lax.fori_loop(0, UNIQ // 16, put, 0)
    outgoing_ref[...] = wide_ref[...].astype(bf16)
    grads_out.wait()
    factors_out.wait()


def layer(pos, pooled, count_a, count_b, returned, target, weight, out_weight):
    return pl.pallas_call(
        layer_kernel,
        out_shape=(
            shape((BAGS, EMB), f32),
            shape((SLOTS, EMB), bf16),
            shape((2, B_DEV, HID), bf16),
            shape((1, HID), f32),
        ),
        in_specs=[SMEM, VMEM, HBM, HBM, VMEM, VMEM, HBM, VMEM],
        out_specs=[HBM, VMEM, HBM, VMEM],
        scratch_shapes=[
            pltpu.VMEM((SLOTS, EMB), f32),
            pltpu.VMEM((UNIQ, EMB), f32),
            pltpu.VMEM((BAGS, UNIQ), bf16),
            pltpu.VMEM((HID, HID), bf16),
            pltpu.VMEM((BAGS, EMB), f32),
            pltpu.VMEM((2, B_DEV, HID), bf16),
            pltpu.SemaphoreType.DMA((5,)),
        ],
        compiler_params=params(50),
        cost_estimate=cost(4 * 10**9, 20 * MIB),
        name="layer",
    )(pos, pooled, count_a, count_b, returned, target, weight, out_weight)


def hidden_kernel(mine_ref, one_ref, two_ref, hidden_ref):
    at = lax.broadcasted_iota(i32, (1, HID // 2), 1) ^ mine_ref[0]
    x_high, y_high = (at >> 8) & 1, (at >> 6) & 1
    x = 2 * x_high + (x_high ^ ((at >> 7) & 1))
    y = 2 * y_high + (y_high ^ ((at >> 5) & 1))
    source = ((((at >> 2) & 7) * 4 + x) * 2 + (at >> 9)) * 16 + y * 4 + (at & 3)
    order = (lax.broadcasted_iota(i32, (HID, HID // 2), 0) == source).astype(f32).astype(bf16)
    total = mm_tn(mm(one_ref[0], order).astype(bf16), one_ref[1])
    hidden_ref[...] = total + mm_tn(mm(two_ref[0], order).astype(bf16), two_ref[1])


def hidden_half(mine, one, two):
    return pl.pallas_call(
        hidden_kernel,
        out_shape=shape((HID // 2, HID), f32),
        in_specs=[SMEM, VMEM, VMEM],
        out_specs=VMEM,
        compiler_params=params(24),
        cost_estimate=cost(4 * 10**9, 4 * MIB),
        name="hidden_half",
    )(mine, one, two)


def scatter_kernel(
    look_ref,
    clash_ref,
    flat_ref,
    mine_ref,
    bag_ref,
    grad_ref,
    keep_ref,
    send_ref,
    acc_ref,
    halves_ref,
    rows_ref,
    grad_vmem,
    keep_vmem,
    send_vmem,
    sems,
):
    grads_in = pltpu.make_async_copy(grad_ref, grad_vmem, sems.at[0, 0])
    grads_in.start()
    grads_in.wait()
    grads = grad_vmem[...]
    high, low = split(grads)
    halves_ref[:, 0:EMB] = high
    halves_ref[:, EMB:] = low

    def stage(q, _):
        for j in range(BATCH):
            k = q * BATCH + j
            start, in_bag = bags_of(flat_ref, bag_ref, k)
            both = mm_tn(in_bag, halves_ref[pl.ds(start, WINDOW), :])
            rows_ref[pl.ds(pl.multiple_of(k * BLOCK, BLOCK), BLOCK), :] = (
                both[:, :EMB] + both[:, EMB:]
            )
        acc_rows = HOT // (BLOCKS // BATCH)
        for j in range(acc_rows // 512):
            acc_ref[pl.ds(pl.multiple_of(q * acc_rows + j * 512, 512), 512), :] = jnp.zeros(
                (512, EMB), f32
            )
        return 0

    lax.fori_loop(0, BLOCKS // BATCH, stage, 0)

    def distinct(at):
        rows = [look_ref[at + m] for m in range(GROUP)]
        sums = [
            acc_ref[pl.ds(rows[m], 1), :] + rows_ref[pl.ds(at + m, 1), :] for m in range(GROUP)
        ]
        for m in range(GROUP):
            acc_ref[pl.ds(rows[m], 1), :] = sums[m]

    def block(k, _):
        clashes = clash_ref[k * FLAGS + ANY]

        @pl.when(clashes == 0)
        def _():
            def pair(q, _):
                distinct(k * 128 + q * 2 * GROUP)
                distinct(k * 128 + q * 2 * GROUP + GROUP)
                return 0

            lax.fori_loop(0, 128 // GROUP // 2, pair, 0)

        @pl.when(clashes != 0)
        def _():
            def group(q, _):
                at = k * 128 + q * GROUP
                clash = clash_ref[k * FLAGS + q]

                @pl.when(clash == 0)
                def _():
                    distinct(at)

                @pl.when(clash != 0)
                def _():
                    for m in range(GROUP):
                        acc_ref[pl.ds(look_ref[at + m], 1), :] += rows_ref[pl.ds(at + m, 1), :]

                return 0

            lax.fori_loop(0, 128 // GROUP, group, 0)

        return 0

    lax.fori_loop(0, LOOK // 128, block, 0)

    core, bits = mine_ref[1], mine_ref[2]

    def copies(s):
        return (
            pltpu.make_async_copy(send_vmem.at[s % 2], send_ref.at[s], sems.at[s % 2, 0]),
            pltpu.make_async_copy(keep_vmem.at[s % 2], keep_ref.at[s], sems.at[s % 2, 1]),
        )

    for s in range(4):
        if s >= 2:
            for copy in copies(s - 2):
                copy.wait()

        def gather(k, _, s=s):
            bit = [(bits >> (3 - axis)) & 1 for axis in range(4)]
            for j, axis in enumerate(ORDERS[s]):
                bit[axis] = bit[axis] ^ ((k >> (3 - j)) & 1)
            x = 2 * bit[0] + (bit[0] ^ bit[1])
            y = 2 * bit[2] + (bit[2] ^ bit[3])
            base = x * 1024 + y * 128 + 32 * s
            own = pl.multiple_of(base + 512 * core, 32)
            other = pl.multiple_of(base + 512 * (1 - core), 32)
            for z in range(8):
                keep_vmem[s % 2, k, z] = acc_ref[pl.ds(own + z * 4096, 32), :]
                send_vmem[s % 2, k, z] = acc_ref[pl.ds(other + z * 4096, 32), :].astype(bf16)
            return 0

        lax.fori_loop(0, 16, gather, 0)
        for copy in copies(s):
            copy.start()
    for s in (2, 3):
        for copy in copies(s):
            copy.wait()


def scatter_hot(look, clash, flat, mine, bags, grads):
    return pl.pallas_call(
        scatter_kernel,
        out_shape=(shape((4, 16, 8, 32, EMB), f32), shape((4, 16, 8, 32, EMB), bf16)),
        in_specs=[SMEM] * 4 + [VMEM, HBM],
        out_specs=[HBM] * 2,
        scratch_shapes=[
            pltpu.VMEM((HOT + GROUP, EMB), f32),
            pltpu.VMEM((BAGS, 2 * EMB), bf16),
            pltpu.VMEM((LOOK, EMB), f32),
            pltpu.VMEM((BAGS, EMB), f32),
            pltpu.VMEM((2, 16, 8, 32, EMB), f32),
            pltpu.VMEM((2, 16, 8, 32, EMB), bf16),
            pltpu.SemaphoreType.DMA((2, 2)),
        ],
        compiler_params=params(58),
        cost_estimate=cost(10**9, 80 * MIB),
        name="scatter",
    )(look, clash, flat, mine, bags, grads)


def split(values):
    high = values.astype(bf16)
    return high, (values - high.astype(f32)).astype(bf16)


def hot_parts(count):
    return 2 if count <= 2 else 1


def put_hot(send_ref, count, at, total):
    if hot_parts(count) == 2:
        high, low = split(total)
        send_ref[count * 256 + at * 256 : count * 256 + at * 256 + 256, :] = low
    else:
        high = total.astype(bf16)
    send_ref[at * 256 : at * 256 + 256, :] = high


def get_hot(recv_ref, count, at):
    high = recv_ref[at * 256 : at * 256 + 256, :].astype(f32)
    if hot_parts(count) == 2:
        base = count * 256 + at * 256
        high = high + recv_ref[base : base + 256, :].astype(f32)
    return high


def hidden_base(count):
    return count * 256 * hot_parts(count)


def put_hidden(send_ref, count, at, total):
    high, low = split(total)
    base = hidden_base(count) + at * 128
    for part, values in enumerate((high, low)):
        for half in range(2):
            row = base + part * 64 + half * 32
            send_ref[row : row + 32, :] = values[:, half * 128 : half * 128 + 128]


def get_hidden(recv_ref, count, at):
    base = hidden_base(count) + at * 128
    pieces = [recv_ref[base + 32 * q : base + 32 * q + 32, :].astype(f32) for q in range(4)]
    return jnp.concatenate([pieces[0] + pieces[2], pieces[1] + pieces[3]], axis=1)


def out_base(count):
    return hidden_base(count) + count * 128


def put_out(send_ref, count, total):
    high = total.astype(bf16).astype(f32)
    send_ref[out_base(count) : out_base(count) + 16, :] = jnp.concatenate(
        [high, total - high], axis=0
    ).astype(bf16)


def get_out(recv_ref, count):
    wide = recv_ref[out_base(count) : out_base(count) + 16, :].astype(f32)
    return wide[0:8] + wide[8:16]


def rounded_out(total):
    high = total.astype(bf16).astype(f32)
    return high + (total - high).astype(bf16).astype(f32)


def place_of(s, step, k):
    left = sorted(ORDERS[s][step:])
    bit = len(left) - 1 - left.index(ORDERS[s][step])
    rest = ((k >> (bit + 1)) << bit) | (k & ((1 << bit) - 1))
    return (k >> bit) & 1, rest


def send_shapes(count):
    return tuple(
        shape((out_base(count) + (16 if s == 0 else 0), EMB), bf16) for s in range(4)
    ) + (shape((8, EMB), f32),)


def keep_shapes(count):
    return tuple(shape((count, 8, 32, EMB), f32) for s in range(4)) + tuple(
        shape((count, 32, 256), f32) for s in range(4)
    )


def first_send_kernel(keep_ref, recv_ref, hidden_ref, out_ref, out_recv_ref, *outs):
    for s in range(4):

        def hot(k, _, s=s):
            total = keep_ref[s, k + 8].reshape(256, EMB) + recv_ref[s, k + 8].astype(f32).reshape(
                256, EMB
            )
            outs[s][pl.ds(pl.multiple_of(k * 256, 256), 256), :] = total.astype(bf16)
            return 0

        lax.fori_loop(0, 8, hot, 0)
        for k in range(16):
            flag, rest = place_of(s, 0, k)
            if flag:
                put_hidden(
                    outs[s], 8, rest, hidden_ref[32 * k : 32 * k + 32, 256 * s : 256 * s + 256]
                )
    total = out_ref[...] + out_recv_ref[...]
    outs[4][...] = total
    put_out(outs[0], 8, total)


def first_send(keep, recv, hidden, out, out_recv):
    return pl.pallas_call(
        first_send_kernel,
        out_shape=send_shapes(8),
        in_specs=[VMEM] * 5,
        out_specs=[VMEM] * 5,
        compiler_params=params(24),
        cost_estimate=cost(10**6, 12 * MIB),
        name="first_send",
    )(keep, recv, hidden, out, out_recv)


def first_keep_kernel(keep_ref, recv_ref, hidden_ref, *outs):
    for s in range(4):

        def hot(k, _, s=s):
            outs[s][k] = keep_ref[s, k] + recv_ref[s, k].astype(f32)
            return 0

        lax.fori_loop(0, 8, hot, 0)
        for k in range(16):
            flag, rest = place_of(s, 0, k)
            if not flag:
                outs[4 + s][rest] = hidden_ref[32 * k : 32 * k + 32, 256 * s : 256 * s + 256]


def first_keep(keep, recv, hidden):
    return pl.pallas_call(
        first_keep_kernel,
        out_shape=keep_shapes(8),
        in_specs=[VMEM] * 3,
        out_specs=[VMEM] * 8,
        compiler_params=params(24),
        cost_estimate=cost(10**6, 12 * MIB),
        name="first_keep",
    )(keep, recv, hidden)


def next_kernel(step, *refs):
    count = 16 >> step
    recvs, out_ref, hots, hiddens = refs[0:4], refs[4], refs[5:9], refs[9:13]
    sends, out_new_ref, hot_outs, hidden_outs = refs[13:17], refs[17], refs[18:22], refs[22:26]
    for s in range(4):
        for k in range(count):
            total = hots[s][k].reshape(256, EMB) + get_hot(recvs[s], count, k)
            if k >= count // 2:
                put_hot(sends[s], count // 2, k - count // 2, total)
            else:
                hot_outs[s][k] = total.reshape(8, 32, EMB)
            flag, rest = place_of(s, step, k)
            hidden = hiddens[s][k] + get_hidden(recvs[s], count, k)
            if flag:
                put_hidden(sends[s], count // 2, rest, hidden)
            else:
                hidden_outs[s][rest] = hidden
    total = rounded_out(out_ref[...]) + get_out(recvs[0], count)
    out_new_ref[...] = total
    put_out(sends[0], count // 2, total)


def next_step(step, sends, keeps):
    count = 16 >> step
    values = pl.pallas_call(
        lambda *refs: next_kernel(step, *refs),
        out_shape=send_shapes(count // 2) + keep_shapes(count // 2),
        in_specs=[VMEM] * 13,
        out_specs=[VMEM] * 13,
        compiler_params=params(24),
        cost_estimate=cost(10**6, count * 2 * MIB),
        name="step_" + str(step + 1),
    )(*sends, *keeps)
    return values[:5], values[5:]


Z_ROWS = 336


def last_kernel(*refs):
    recvs, sum_ref, hots, hiddens, out_ref, pieces_ref = (
        refs[0:4], refs[4], refs[5:9], refs[9:13], refs[13], refs[14],
    )
    for s in range(4):
        total = hots[s][0].reshape(256, EMB) + get_hot(recvs[s], 1, 0)
        hidden = hiddens[s][0] + get_hidden(recvs[s], 1, 0)
        high, low = split(total)
        for z in range(8):
            out_ref[z, 32 * s : 32 * s + 32, :] = high[32 * z : 32 * z + 32]
            out_ref[z, 128 + 32 * s : 160 + 32 * s, :] = low[32 * z : 32 * z + 32]
            for half in range(2):
                row = (2 * s + half) * 4
                pieces_ref[z, row : row + 4, :] = hidden[
                    4 * z : 4 * z + 4, half * 128 : half * 128 + 128
                ]
    total = rounded_out(sum_ref[...]) + get_out(recvs[0], 1)
    high = total.astype(bf16).astype(f32)
    both = jnp.concatenate([high, total - high], axis=0).astype(bf16)
    for z in range(8):
        high, low = split(pieces_ref[z])
        out_ref[z, 256:288, :] = high
        out_ref[z, 288:320, :] = low
        out_ref[z, 320:336, :] = both


def last_step(sends, keeps):
    return pl.pallas_call(
        last_kernel,
        out_shape=shape((8, Z_ROWS, EMB), bf16),
        in_specs=[VMEM] * 13,
        out_specs=VMEM,
        scratch_shapes=[pltpu.VMEM((8, 32, EMB), f32)],
        compiler_params=params(16),
        cost_estimate=cost(10**6, 2 * MIB),
        name="step_5",
    )(*sends, *keeps)


def row_update(param, accum_row, grad):
    turned = grad.T
    accum_new = accum_row + jnp.sum(turned * turned, axis=0, keepdims=True) * (1.0 / EMB)
    return param - (learn_rate * turned / jnp.sqrt(accum_new)).T, accum_new


def update_kernel(
    place_ref,
    recv_ref,
    slab_ref,
    accum_ref,
    weight_ref,
    hid_accum_ref,
    out_weight_ref,
    out_accum_ref,
    new_ref,
    accum_new_ref,
    weight_new_ref,
    hid_new_ref,
    out_new_ref,
    out_accum_new_ref,
    out_ref,
):
    total = jnp.sum(recv_ref[...].astype(f32), axis=0)
    new_ref[...], accum_new_ref[...] = row_update(
        slab_ref[...].astype(f32), accum_ref[...], total[0:128] + total[128:256]
    )
    hidden = total[256:288] + total[288:320]
    for part in range(8):
        columns = slice(part * 128, part * 128 + 128)
        grad = hidden[part * 4 : part * 4 + 4]
        accum_new = hid_accum_ref[:, columns] + grad * grad
        hid_new_ref[:, columns] = accum_new
        weight_new_ref[:, columns] = weight_ref[:, columns] - learn_rate * grad / jnp.sqrt(accum_new)
    out_ref[...] = total[320:328] + total[328:336]
    row = out_ref[pl.ds(place_ref[1], 1), :]
    grad = pltpu.roll(row, place_ref[2], 1)[:, 0:4]
    accum_new = out_accum_ref[...] + grad * grad
    out_accum_new_ref[...] = accum_new
    out_new_ref[...] = out_weight_ref[...] - learn_rate * grad / jnp.sqrt(accum_new)


def update_owned(place, recv, slab, accum, weight, hid_accum, out_weight, out_accum):
    return pl.pallas_call(
        update_kernel,
        out_shape=(
            shape((128, EMB), f32),
            shape((1, 128), f32),
            shape((4, HID), f32),
            shape((4, HID), f32),
            shape((1, 4), f32),
            shape((1, 4), f32),
        ),
        in_specs=[SMEM] + [VMEM] * 7,
        out_specs=[VMEM] * 6,
        scratch_shapes=[pltpu.VMEM((8, EMB), f32)],
        compiler_params=params(16),
        name="update",
    )(place, recv, slab, accum, weight, hid_accum, out_weight, out_accum)


def cold_grad_kernel(asked_ref, incoming_ref, a_ref, b_ref):
    asked = asked_ref[...]
    incoming = incoming_ref[...]
    for part in range(8):
        rows = lax.broadcasted_iota(i32, (256, SLOTS), 0) + part * 256
        total = mm((rows == asked).astype(f32).astype(bf16), incoming).astype(bf16)
        if part < 4:
            a_ref[part * 256 : part * 256 + 256, :] = total
        else:
            b_ref[part * 256 - 1024 : part * 256 - 768, :] = total


def cold_grads(asked, incoming):
    return pl.pallas_call(
        cold_grad_kernel,
        out_shape=(shape((1024, EMB), bf16),) * 2,
        in_specs=[VMEM] * 2,
        out_specs=[VMEM] * 2,
        compiler_params=params(24),
        cost_estimate=cost(2 * 10**9, 4 * MIB),
        name="cold_grads",
    )(asked, incoming)


def pair_kernel(a, b, c, d, e_ref, f_ref):
    e_ref[...] = (a[...].astype(f32) + b[...].astype(f32)).astype(bf16)
    f_ref[...] = (c[...].astype(f32) + d[...].astype(f32)).astype(bf16)


def pair_sums(a, b, c, d):
    return pl.pallas_call(
        pair_kernel,
        out_shape=(shape((1024, EMB), bf16),) * 2,
        in_specs=[VMEM] * 4,
        out_specs=[VMEM] * 2,
        compiler_params=params(16),
        name="pair_sums",
    )(a, b, c, d)


def cold_update_kernel(a, b, c, d, table_ref, accum_ref, new_ref, accum_new_ref):
    for block in range(16):
        one, two = (a, b) if block < 8 else (c, d)
        at = slice((block % 8) * 128, (block % 8) * 128 + 128)
        rows = slice(block * 128, block * 128 + 128)
        grad = one[at, :].astype(f32) + two[at, :].astype(f32)
        new_ref[rows, :], accum_new_ref[block : block + 1, :] = row_update(
            table_ref[rows, :], accum_ref[block : block + 1, :], grad
        )


def update_cold(a, b, c, d, table, accum):
    return pl.pallas_call(
        cold_update_kernel,
        out_shape=(shape((R_OWN, EMB), f32), shape((R_OWN // 128, 128), f32)),
        in_specs=[VMEM] * 6,
        out_specs=[VMEM] * 2,
        compiler_params=params(16),
        name="cold_update",
    )(a, b, c, d, table, accum)


def dp_index(z, x, core):
    return (z * 4 + x) * 2 + core


def over_core(value):
    pairs = [
        (dp_index(z, x, core), dp_index(z, x, 1 - core))
        for z in range(8)
        for x in range(4)
        for core in range(2)
    ]
    return lax.ppermute(value, "dp", pairs)


def over_axis(value, axis):
    swap = (lambda i: 3 - i) if axis in (0, 2) else (lambda i: i ^ 1)
    if axis >= 2:
        return lax.ppermute(value, "rep", [(y, swap(y)) for y in range(4)])
    pairs = [
        (dp_index(z, x, core), dp_index(z, swap(x), core))
        for z in range(8)
        for x in range(4)
        for core in range(2)
    ]
    return lax.ppermute(value, "dp", pairs)


Z_GROUPS = [[dp_index(z, x, core) for z in range(8)] for x in range(4) for core in range(2)]


def over_z(value):
    return lax.all_to_all(
        value, "dp", split_axis=0, concat_axis=0, tiled=True, axis_index_groups=Z_GROUPS
    )


def on_device(
    hot_slab,
    hot_accum,
    cold_table,
    cold_accum,
    touched_owner,
    touched_row,
    lookup_index,
    bag_id,
    labels,
    w_hidden,
    hidden_accum,
    w_out,
    out_accum,
):
    dp = lax.axis_index("dp")
    y = lax.axis_index("rep")
    core, x = dp & 1, (dp >> 1) & 3
    position = dp * 4 + y
    bits = ((x ^ (x >> 1)) << 2) | (y ^ (y >> 1))
    place = jnp.stack([position * 128, position >> 5, (128 - (position & 31) * 4) & 127]).astype(i32)
    mine = jnp.stack([(core << 9) | (bits << 5), core, bits]).astype(i32)

    rows = LOOK // 128
    look_rows = lookup_index.reshape(rows, 128)
    bag_flat = bag_id.reshape(LOOK)
    bag_rows = bag_id.reshape(rows, 128)

    requests, pos = route(touched_owner.reshape(1, UNIQ), touched_row.reshape(1, UNIQ))
    pos_flat = pos.reshape(UNIQ)
    look_hot, clash = clashes(look_rows)
    look_flat, clash = look_hot.reshape(LOOK), clash.reshape(rows * FLAGS)
    count_a = slot_counts(bag_flat, look_rows, bag_rows)
    asked = lax.all_to_all(requests, "dp", split_axis=0, concat_axis=0, tiled=True)
    asked, count_a, mine, place, clash, pos_flat, look_flat = lax.optimization_barrier(
        (asked, count_a, mine, place, clash, pos_flat, look_flat)
    )
    found = found_rows(asked, cold_table)
    returned = lax.all_to_all(
        found.reshape(N_DP, CAP, EMB), "dp", split_axis=0, concat_axis=0, tiled=True
    ).reshape(SLOTS, EMB)
    pooled, count_b = pool_hot(bag_flat, look_flat, look_rows, bag_rows, hot_slab)
    pooled, count_b, asked_row = lax.optimization_barrier(
        (pooled, count_b, asked.reshape(1, SLOTS))
    )
    bag_grad, outgoing, factors, out_grad = layer(
        pos_flat,
        pooled,
        count_a,
        count_b,
        returned,
        labels.reshape(1, B_DEV),
        w_hidden,
        w_out.reshape(1, HID),
    )
    incoming = lax.all_to_all(
        outgoing.reshape(N_DP, CAP, EMB), "dp", split_axis=0, concat_axis=0, tiled=True
    ).reshape(SLOTS, EMB)
    other_factors = over_core(factors)
    out_grad = out_grad.reshape(8, EMB)
    out_recv = over_core(out_grad)
    keep, send = scatter_hot(look_flat, clash, bag_flat, mine, bag_rows, bag_grad)
    send, incoming, other_factors, out_recv = lax.optimization_barrier(
        (send, incoming, other_factors, out_recv)
    )
    recv = over_core(send)
    cold_a, cold_b = cold_grads(asked_row, incoming)
    recv_a, recv_b = over_axis(cold_a, 3), over_axis(cold_b, 2)
    hidden = hidden_half(mine, factors, other_factors)
    sends = first_send(keep, recv, hidden, out_grad, out_recv)
    recv_a, recv_b, *sends = lax.optimization_barrier((recv_a, recv_b, *sends))
    keeps = first_keep(keep, recv, hidden)
    for step in range(4):
        travelled = [over_axis(sends[s], ORDERS[s][step]) for s in range(4)] + [sends[4]]
        if step < 3:
            sends, keeps = next_step(step + 1, travelled, keeps)
    parts = last_step(travelled, keeps)
    pair_a, pair_b = pair_sums(cold_a, recv_a, cold_b, recv_b)
    parts, pair_a, pair_b = lax.optimization_barrier((parts, pair_a, pair_b))
    recv_a, recv_b = over_axis(pair_a, 2), over_axis(pair_b, 3)
    parts = over_z(parts)
    cold_new, cold_accum_new = update_cold(
        pair_a, recv_a, pair_b, recv_b, cold_table, cold_accum.reshape(R_OWN // 128, 128)
    )

    own_slab = lax.dynamic_slice_in_dim(hot_slab, position * 128, 128, 0)
    own_hidden = lax.dynamic_slice_in_dim(w_hidden, position * 4, 4, 0).astype(f32)
    own_out = lax.dynamic_slice_in_dim(w_out, position * 4, 4, 0)
    hot_new, hot_accum_new, hidden_new, hidden_accum_new, out_new, out_accum_new = update_owned(
        place,
        parts,
        own_slab,
        hot_accum.reshape(1, 128),
        own_hidden,
        hidden_accum,
        own_out.reshape(1, 4),
        out_accum.reshape(1, 4),
    )
    return (
        hot_new,
        hot_accum_new.reshape(128),
        cold_new,
        cold_accum_new.reshape(R_OWN),
        hidden_new,
        hidden_accum_new,
        out_new.reshape(4),
        out_accum_new.reshape(4),
    )


def solution(mesh):
    both = ("dp", "rep")
    in_specs = (
        P(),
        P(both),
        P("dp", None),
        P("dp"),
        P(both, None),
        P(both),
        P(both),
        P(both, None),
        P(both),
        P(),
        P(both, None),
        P(),
        P(both),
    )
    out_specs = (
        P(both, None),
        P(both),
        P("dp", None),
        P("dp"),
        P(both, None),
        P(both, None),
        P(both),
        P(both),
    )
    return jax.shard_map(
        on_device, mesh=mesh, in_specs=in_specs, out_specs=out_specs, check_vma=False
    )
```

```python
import jax
import jax.numpy as jnp
from jax import lax
from jax.experimental import pallas as pl
from jax.experimental.pallas import tpu as pltpu
from jax.sharding import PartitionSpec as P

learn_rate = 0.05
bf16 = jnp.bfloat16
f32 = jnp.float32
i32 = jnp.int32

EMB = 128
HOT = 32768
FEAT = 8
HID = 1024
B_DEV = 256
BAGS = 2048
LOOK = 8192
UNIQ = 1024
CAP = 48
R_OWN = 2048
N_DP = 64
SLOTS = N_DP * CAP
GROUP = 16
BLOCK = 256
WINDOW = BLOCK + 16
BLOCKS = LOOK // BLOCK
BATCH = 4
FLAGS = 128
ANY = FLAGS - 1
LAST_START = BAGS - WINDOW
CUT = 384
ONE = 32704.0
REST = 16384.0
i16 = jnp.int16
MIB = 1 << 20

ORDERS = ((3, 2, 1, 0), (2, 3, 0, 1), (1, 0, 3, 2), (0, 1, 2, 3))

SMEM = pl.BlockSpec(memory_space=pltpu.SMEM)
VMEM = pl.BlockSpec(memory_space=pltpu.VMEM)
HBM = pl.BlockSpec(memory_space=pltpu.HBM)


def params(mib):
    return pltpu.CompilerParams(vmem_limit_bytes=mib * MIB)


def cost(flops, data):
    return pl.CostEstimate(flops=flops, bytes_accessed=data, transcendentals=0)


def shape(dims, dtype):
    return jax.ShapeDtypeStruct(dims, dtype)


def mm(a, b):
    return jnp.dot(a, b, preferred_element_type=f32)


def mm_nt(a, b):
    return lax.dot_general(a, b, (((1,), (1,)), ((), ())), preferred_element_type=f32)


def mm_tn(a, b):
    return lax.dot_general(a, b, (((0,), (0,)), ((), ())), preferred_element_type=f32)


def route_kernel(owner_ref, row_ref, request_ref, pos_ref):
    owner = owner_ref[...]
    row = row_ref[...]
    member = lax.broadcasted_iota(i32, (N_DP, UNIQ), 0) == owner
    ones = member.astype(f32).astype(bf16)
    upper = lax.broadcasted_iota(i32, (UNIQ, UNIQ), 0) < lax.broadcasted_iota(
        i32, (UNIQ, UNIQ), 1
    )
    before = mm(ones, upper.astype(f32).astype(bf16))
    within = jnp.sum(jnp.where(member, before, 0.0), axis=0, keepdims=True).astype(i32)
    pos_ref[...] = owner * CAP + within
    place = (lax.broadcasted_iota(i32, (CAP, UNIQ), 0) == within).astype(f32).astype(bf16)
    high = jnp.where(member, (row >> 6).astype(f32), 0.0).astype(bf16)
    low = jnp.where(member, (row & 63).astype(f32), 0.0).astype(bf16)
    total = mm_nt(high, place) * 64.0 + mm_nt(low, place)
    request_ref[...] = total.astype(i32)


def route(owner, row):
    return pl.pallas_call(
        route_kernel,
        out_shape=(shape((N_DP, CAP), i32), shape((1, UNIQ), i32)),
        in_specs=[VMEM] * 2,
        out_specs=[VMEM] * 2,
        compiler_params=params(16),
        name="route",
    )(owner, row)


def clash_kernel(look_ref, hot_ref, clash_ref):
    rows = LOOK // 128
    lane = lax.broadcasted_iota(i32, (rows, 128), 1) & (GROUP - 1)
    look = look_ref[...]
    look = jnp.where(look < HOT, look, HOT + lane)
    hot_ref[...] = look
    clash = jnp.zeros((rows, 128), f32)
    for shift in range(1, GROUP):
        same = (look == pltpu.roll(look, shift, 1)) & (lane >= shift)
        clash = jnp.maximum(clash, same.astype(f32))
    group = lax.broadcasted_iota(i32, (128, FLAGS), 0) // GROUP
    column = lax.broadcasted_iota(i32, (128, FLAGS), 1)
    gather = (group == column) | (column == ANY)
    clash_ref[...] = mm(clash.astype(bf16), gather.astype(f32).astype(bf16)).astype(i32)


def clashes(look):
    return pl.pallas_call(
        clash_kernel,
        out_shape=(shape((LOOK // 128, 128), i32), shape((LOOK // 128, FLAGS), i32)),
        in_specs=[VMEM],
        out_specs=[VMEM] * 2,
        compiler_params=params(16),
        name="clashes",
    )(look)


def found_kernel(asked_ref, table_ref, found_ref, rows_ref):
    def body(owner, _):
        for j in range(CAP):
            rows_ref[pl.ds(owner * CAP + j, 1), :] = table_ref[pl.ds(asked_ref[owner, j], 1), :]
        return 0

    lax.fori_loop(0, N_DP, body, 0)
    found_ref[...] = rows_ref[...].astype(bf16)


def found_rows(asked, table):
    return pl.pallas_call(
        found_kernel,
        out_shape=shape((SLOTS, EMB), bf16),
        in_specs=[SMEM, VMEM],
        out_specs=VMEM,
        scratch_shapes=[pltpu.VMEM((SLOTS, EMB), f32)],
        compiler_params=params(16),
        name="found",
    )(asked, table)


def one_hot(height, middle, numbers):
    place = lax.broadcasted_iota(i32, (height, numbers.shape[1]), 0) - middle
    place = place.astype(f32).astype(bf16)
    inside = (numbers >= 0) & (numbers < height)
    named = jnp.where(inside, numbers - middle, -middle - 2).astype(f32).astype(bf16)
    return jnp.where(place == named, jnp.ones((), bf16), jnp.zeros((), bf16))


def bags_of(flat_ref, bag_ref, k):
    start = jnp.minimum((flat_ref[k * BLOCK] // 16) * 16, LAST_START)
    start = pl.multiple_of(start, 16)
    in_bag = [one_hot(WINDOW, WINDOW // 2, bag_ref[pl.ds(2 * k + j, 1), :] - start) for j in range(2)]
    return start, jnp.concatenate(in_bag, axis=1)


def count_slots(base, flat_ref, look_ref, bag_ref, acc_ref):
    acc_ref[...] = jnp.zeros_like(acc_ref)
    many = acc_ref.shape[1]

    def body(q, _):
        parts = []
        for b in range(BATCH):
            k = BATCH * q + b
            start, in_bag = bags_of(flat_ref, bag_ref, k)
            in_slot = []
            for j in range(2):
                slots = look_ref[pl.ds(2 * k + j, 1), :] - (HOT + base)
                pieces = [one_hot(128, 64, slots - at) for at in range(0, many, 128)]
                in_slot.append(jnp.concatenate(pieces, axis=0))
            in_slot = jnp.concatenate(in_slot, axis=1)
            parts.append((start, mm_nt(in_bag, in_slot).astype(bf16)))
        for start, part in parts:
            acc_ref[pl.ds(start, WINDOW), :] += part
        return 0

    lax.fori_loop(0, BLOCKS // BATCH, body, 0)


def counts_out(acc_ref, counts_ref, sems):
    return [
        pltpu.make_async_copy(
            acc_ref.at[pl.ds(c * 512, 512)], counts_ref.at[pl.ds(c * 512, 512)], sems.at[c]
        )
        for c in range(4)
    ]


def counts_kernel(flat_ref, look_ref, bag_ref, counts_ref, acc_ref, sems):
    count_slots(0, flat_ref, look_ref, bag_ref, acc_ref)
    copies = counts_out(acc_ref, counts_ref, sems)
    for copy in copies:
        copy.start()
    for copy in copies:
        copy.wait()


def slot_counts(flat, look, bags):
    return pl.pallas_call(
        counts_kernel,
        out_shape=shape((BAGS, CUT), bf16),
        in_specs=[SMEM, VMEM, VMEM],
        out_specs=HBM,
        scratch_shapes=[pltpu.VMEM((BAGS, CUT), bf16), pltpu.SemaphoreType.DMA((4,))],
        compiler_params=params(58),
        cost_estimate=cost(5 * 10**9, 8 * MIB),
        name="counts",
    )(flat, look, bags)


CHUNKS = 8


def pool_kernel(
    flat_ref,
    look_ref,
    raw_ref,
    bag_ref,
    slab_ref,
    pooled_ref,
    counts_ref,
    slab_vmem,
    table_ref,
    rows_ref,
    counts_vmem,
    sems,
    count_sems,
):
    height = HOT // CHUNKS

    def copy(c):
        rows = pl.ds(c * height, height)
        return pltpu.make_async_copy(slab_ref.at[rows], slab_vmem.at[rows], sems.at[c])

    for c in range(CHUNKS):
        copy(c).start()
    count_slots(CUT, flat_ref, raw_ref, bag_ref, counts_vmem)
    out_copies = counts_out(counts_vmem, counts_ref, count_sems)
    for out_copy in out_copies:
        out_copy.start()
    pooled_ref[...] = jnp.zeros_like(pooled_ref)
    table_ref[HOT:, :] = jnp.zeros((GROUP, EMB), f32)
    for c in range(CHUNKS):
        copy(c).wait()

        def widen(q, _, c=c):
            rows = pl.ds(pl.multiple_of(c * height + q * 512, 512), 512)
            table_ref[rows, :] = slab_vmem[rows, :].astype(f32)
            return 0

        lax.fori_loop(0, height // 512, widen, 0)

    def gather(q, _):
        for j in range(32):
            at = q * 32 + j
            rows_ref[pl.ds(at, 1), :] = table_ref[pl.ds(look_ref[at], 1), :]
        return 0

    lax.fori_loop(0, LOOK // 32, gather, 0)

    def batch(q, _):
        parts = []
        for j in range(BATCH):
            k = q * BATCH + j
            start, in_bag = bags_of(flat_ref, bag_ref, k)
            rows = rows_ref[pl.ds(pl.multiple_of(k * BLOCK, BLOCK), BLOCK), :].astype(bf16)
            parts.append((start, mm(in_bag, rows)))
        for start, part in parts:
            pooled_ref[pl.ds(start, WINDOW), :] += part
        return 0

    lax.fori_loop(0, BLOCKS // BATCH, batch, 0)
    for out_copy in out_copies:
        out_copy.wait()


def pool_hot(flat, look, raw, bags, slab):
    return pl.pallas_call(
        pool_kernel,
        out_shape=(shape((BAGS, EMB), f32), shape((BAGS, UNIQ - CUT), bf16)),
        in_specs=[SMEM, SMEM, VMEM, VMEM, HBM],
        out_specs=[VMEM, HBM],
        scratch_shapes=[
            pltpu.VMEM((HOT, EMB), bf16),
            pltpu.VMEM((HOT + GROUP, EMB), f32),
            pltpu.VMEM((LOOK, EMB), f32),
            pltpu.VMEM((BAGS, UNIQ - CUT), bf16),
            pltpu.SemaphoreType.DMA((CHUNKS,)),
            pltpu.SemaphoreType.DMA((4,)),
        ],
        compiler_params=params(58),
        cost_estimate=cost(10**9, 40 * MIB),
        name="pool",
    )(flat, look, raw, bags, slab)


def layer_kernel(
    pos_ref,
    pooled_ref,
    count_a_ref,
    count_b_ref,
    returned_ref,
    target_ref,
    weight_ref,
    out_weight_ref,
    bag_grad_ref,
    outgoing_ref,
    factors_ref,
    out_grad_ref,
    wide_ref,
    slots_ref,
    counts_vmem,
    weight_vmem,
    grads_vmem,
    factors_vmem,
    sems,
):
    counts_in = [
        pltpu.make_async_copy(count_a_ref, counts_vmem.at[:, pl.ds(0, CUT)], sems.at[0]),
        pltpu.make_async_copy(count_b_ref, counts_vmem.at[:, pl.ds(CUT, UNIQ - CUT)], sems.at[4]),
    ]
    weight_in = pltpu.make_async_copy(weight_ref, weight_vmem, sems.at[1])
    grads_out = pltpu.make_async_copy(grads_vmem, bag_grad_ref, sems.at[2])
    factors_out = pltpu.make_async_copy(factors_vmem, factors_ref, sems.at[3])
    for copy in counts_in:
        copy.start()
    weight_in.start()
    wide_ref[...] = returned_ref[...].astype(f32)

    def fetch(k, _):
        for j in range(16):
            at = k * 16 + j
            slots_ref[pl.ds(at, 1), :] = wide_ref[pl.ds(pos_ref[at], 1), :]
        return 0

    lax.fori_loop(0, UNIQ // 16, fetch, 0)
    for copy in counts_in:
        copy.wait()
    counts = counts_vmem[...]
    grads_vmem[...] = pooled_ref[...] + mm(counts, slots_ref[...].astype(bf16))
    pooled_in = jnp.concatenate(
        [grads_vmem[pl.ds(f, B_DEV, stride=FEAT), :] for f in range(FEAT)], axis=1
    ).astype(bf16)
    weight_in.wait()
    weight = weight_vmem[...]
    out_weight = out_weight_ref[...]
    preact = mm(pooled_in, weight)
    gate = jax.nn.sigmoid(preact)
    act = (preact * gate).astype(bf16).astype(f32)
    logits = jnp.sum(act * out_weight, axis=1, keepdims=True)
    diagonal = lax.broadcasted_iota(i32, (B_DEV, B_DEV), 0) == lax.broadcasted_iota(
        i32, (B_DEV, B_DEV), 1
    )
    target = jnp.sum(jnp.where(diagonal, target_ref[...], 0.0), axis=1, keepdims=True)
    logit_grad = jax.nn.sigmoid(logits) - target
    out_grad_ref[...] = jnp.sum(act * logit_grad, axis=0, keepdims=True)
    act_grad = (logit_grad * out_weight * gate * (1.0 + preact * (1.0 - gate))).astype(bf16)
    factors_vmem[0] = pooled_in
    factors_vmem[1] = act_grad
    factors_out.start()
    input_grad = mm_nt(act_grad, weight)
    for f in range(FEAT):
        grads_vmem[pl.ds(f, B_DEV, stride=FEAT), :] = input_grad[:, f * EMB : (f + 1) * EMB]

    grads_out.start()
    grads = grads_vmem[...]
    high = grads.astype(bf16)
    low = (grads - high.astype(f32)).astype(bf16)
    both = mm_tn(counts, jnp.concatenate([high, low], axis=1))
    slots_ref[...] = both[:, :EMB] + both[:, EMB:]
    wide_ref[...] = jnp.zeros_like(wide_ref)

    def put(k, _):
        for j in range(16):
            at = k * 16 + j
            wide_ref[pl.ds(pos_ref[at], 1), :] = slots_ref[pl.ds(at, 1), :]
        return 0

    lax.fori_loop(0, UNIQ // 16, put, 0)
    outgoing_ref[...] = wide_ref[...].astype(bf16)
    grads_out.wait()
    factors_out.wait()


def layer(pos, pooled, count_a, count_b, returned, target, weight, out_weight):
    return pl.pallas_call(
        layer_kernel,
        out_shape=(
            shape((BAGS, EMB), f32),
            shape((SLOTS, EMB), bf16),
            shape((2, B_DEV, HID), bf16),
            shape((1, HID), f32),
        ),
        in_specs=[SMEM, VMEM, HBM, HBM, VMEM, VMEM, HBM, VMEM],
        out_specs=[HBM, VMEM, HBM, VMEM],
        scratch_shapes=[
            pltpu.VMEM((SLOTS, EMB), f32),
            pltpu.VMEM((UNIQ, EMB), f32),
            pltpu.VMEM((BAGS, UNIQ), bf16),
            pltpu.VMEM((HID, HID), bf16),
            pltpu.VMEM((BAGS, EMB), f32),
            pltpu.VMEM((2, B_DEV, HID), bf16),
            pltpu.SemaphoreType.DMA((5,)),
        ],
        compiler_params=params(50),
        cost_estimate=cost(4 * 10**9, 20 * MIB),
        name="layer",
    )(pos, pooled, count_a, count_b, returned, target, weight, out_weight)


def hidden_kernel(mine_ref, one_ref, two_ref, hidden_ref):
    at = lax.broadcasted_iota(i32, (1, HID // 2), 1) ^ mine_ref[0]
    x_high, y_high = (at >> 8) & 1, (at >> 6) & 1
    x = 2 * x_high + (x_high ^ ((at >> 7) & 1))
    y = 2 * y_high + (y_high ^ ((at >> 5) & 1))
    source = ((((at >> 2) & 7) * 4 + x) * 2 + (at >> 9)) * 16 + y * 4 + (at & 3)
    order = (lax.broadcasted_iota(i32, (HID, HID // 2), 0) == source).astype(f32).astype(bf16)
    total = mm_tn(mm(one_ref[0], order).astype(bf16), one_ref[1])
    hidden_ref[...] = total + mm_tn(mm(two_ref[0], order).astype(bf16), two_ref[1])


def hidden_half(mine, one, two):
    return pl.pallas_call(
        hidden_kernel,
        out_shape=shape((HID // 2, HID), f32),
        in_specs=[SMEM, VMEM, VMEM],
        out_specs=VMEM,
        compiler_params=params(24),
        cost_estimate=cost(4 * 10**9, 4 * MIB),
        name="hidden_half",
    )(mine, one, two)


def diagonal(rows):
    return lax.broadcasted_iota(i32, (rows, 128), 0) == lax.broadcasted_iota(i32, (rows, 128), 1)


def blocks_of(values):
    rows = min(128, values.shape[0])
    return rows, range(values.shape[0] // rows)


def scales_of(values):
    rows = min(128, values.shape[0])
    most = jnp.maximum(jnp.max(jnp.abs(values), axis=1, keepdims=True), 1e-30)
    across = [
        jnp.sum(
            jnp.where(diagonal(rows), most[at : at + rows], 0.0), axis=0, keepdims=True
        )
        for at in range(0, values.shape[0], rows)
    ]
    return most, jnp.concatenate(across, axis=0)


def scaled(values, most):
    return values * (ONE / most)


def unscaled(values, across):
    blocks = across.shape[0]
    rows = values.shape[0] // blocks
    most = [
        jnp.sum(jnp.where(diagonal(rows), across[b : b + 1], 0.0), axis=1, keepdims=True)
        for b in range(blocks)
    ]
    return values * (jnp.concatenate(most, axis=0) * (1.0 / ONE))


def two_integers(across):
    power = jnp.floor(jnp.log(jnp.maximum(across, 1e-30)) * 1.4426950408889634) + 1.0
    return power, across * jnp.exp2(14.0 - power)


def from_two(power, bits):
    return bits * jnp.exp2(power - 14.0)


def nearest(values):
    return (values + 12582912.0) - 12582912.0


def whole(values):
    return nearest(values).astype(i32).astype(i16)


def wide(values):
    return values.astype(i32).astype(f32)


def code(values):
    most, across = scales_of(values)
    return whole(scaled(values, most)), across


def decode_rows(coded, across):
    return unscaled(wide(coded), across)


def code_twice(values):
    most, across = scales_of(values)
    values = scaled(values, most)
    high = nearest(values)
    return whole(jnp.concatenate([high, (values - high) * REST], axis=0)), across


def decode_twice(coded, across):
    coded = wide(coded)
    rows = coded.shape[0] // 2
    return unscaled(coded[:rows] + coded[rows:] * (1.0 / REST), across)


def scatter_kernel(
    look_ref,
    clash_ref,
    flat_ref,
    mine_ref,
    bag_ref,
    grad_ref,
    keep_ref,
    send_ref,
    power_ref,
    acc_ref,
    halves_ref,
    rows_ref,
    grad_vmem,
    keep_vmem,
    send_vmem,
    sems,
):
    grads_in = pltpu.make_async_copy(grad_ref, grad_vmem, sems.at[0, 0])
    grads_in.start()
    grads_in.wait()
    grads = grad_vmem[...]
    high, low = split(grads)
    halves_ref[:, 0:EMB] = high
    halves_ref[:, EMB:] = low

    def stage(q, _):
        for j in range(BATCH):
            k = q * BATCH + j
            start, in_bag = bags_of(flat_ref, bag_ref, k)
            both = mm_tn(in_bag, halves_ref[pl.ds(start, WINDOW), :])
            rows_ref[pl.ds(pl.multiple_of(k * BLOCK, BLOCK), BLOCK), :] = (
                both[:, :EMB] + both[:, EMB:]
            )
        acc_rows = HOT // (BLOCKS // BATCH)
        for j in range(acc_rows // 512):
            acc_ref[pl.ds(pl.multiple_of(q * acc_rows + j * 512, 512), 512), :] = jnp.zeros(
                (512, EMB), f32
            )
        return 0

    lax.fori_loop(0, BLOCKS // BATCH, stage, 0)

    def distinct(at):
        rows = [look_ref[at + m] for m in range(GROUP)]
        sums = [
            acc_ref[pl.ds(rows[m], 1), :] + rows_ref[pl.ds(at + m, 1), :] for m in range(GROUP)
        ]
        for m in range(GROUP):
            acc_ref[pl.ds(rows[m], 1), :] = sums[m]

    def block(k, _):
        clashes = clash_ref[k * FLAGS + ANY]

        @pl.when(clashes == 0)
        def _():
            def pair(q, _):
                distinct(k * 128 + q * 2 * GROUP)
                distinct(k * 128 + q * 2 * GROUP + GROUP)
                return 0

            lax.fori_loop(0, 128 // GROUP // 2, pair, 0)

        @pl.when(clashes != 0)
        def _():
            def group(q, _):
                at = k * 128 + q * GROUP
                clash = clash_ref[k * FLAGS + q]

                @pl.when(clash == 0)
                def _():
                    distinct(at)

                @pl.when(clash != 0)
                def _():
                    for m in range(GROUP):
                        acc_ref[pl.ds(look_ref[at + m], 1), :] += rows_ref[pl.ds(at + m, 1), :]

                return 0

            lax.fori_loop(0, 128 // GROUP, group, 0)

        return 0

    lax.fori_loop(0, LOOK // 128, block, 0)

    core, bits = mine_ref[1], mine_ref[2]

    def copies(s):
        return (
            pltpu.make_async_copy(send_vmem.at[s % 2], send_ref.at[s], sems.at[s % 2, 0]),
            pltpu.make_async_copy(keep_vmem.at[s % 2], keep_ref.at[s], sems.at[s % 2, 1]),
        )

    for s in range(4):
        if s >= 2:
            for copy in copies(s - 2):
                copy.wait()

        def gather(pair, _, s=s):
            rows = []
            for k in (2 * pair, 2 * pair + 1):
                bit = [(bits >> (3 - axis)) & 1 for axis in range(4)]
                for j, axis in enumerate(ORDERS[s]):
                    bit[axis] = bit[axis] ^ ((k >> (3 - j)) & 1)
                x = 2 * bit[0] + (bit[0] ^ bit[1])
                y = 2 * bit[2] + (bit[2] ^ bit[3])
                base = x * 1024 + y * 128 + 32 * s
                own = pl.multiple_of(base + 512 * core, 32)
                other = pl.multiple_of(base + 512 * (1 - core), 32)
                for z in range(8):
                    keep_vmem[s % 2, k, z] = acc_ref[pl.ds(own + z * 4096, 32), :]
                    rows.append(acc_ref[pl.ds(other + z * 4096, 32), :])
            coded, power = code(jnp.concatenate(rows, axis=0))
            send_vmem[s % 2, pl.ds(2 * pair, 2)] = coded.reshape(2, 8, 32, EMB)
            for b in range(4):
                power_ref[pl.ds((s * 8 + pair) * 4 + b, 1), :] = power[b : b + 1]
            return 0

        lax.fori_loop(0, 8, gather, 0)
        for copy in copies(s):
            copy.start()
    for s in (2, 3):
        for copy in copies(s):
            copy.wait()


def scatter_hot(look, clash, flat, mine, bags, grads):
    return pl.pallas_call(
        scatter_kernel,
        out_shape=(
            shape((4, 16, 8, 32, EMB), f32),
            shape((4, 16, 8, 32, EMB), i16),
            shape((128, 128), f32),
        ),
        in_specs=[SMEM] * 4 + [VMEM, HBM],
        out_specs=[HBM, HBM, VMEM],
        scratch_shapes=[
            pltpu.VMEM((HOT + GROUP, EMB), f32),
            pltpu.VMEM((BAGS, 2 * EMB), bf16),
            pltpu.VMEM((LOOK, EMB), f32),
            pltpu.VMEM((BAGS, EMB), f32),
            pltpu.VMEM((2, 16, 8, 32, EMB), f32),
            pltpu.VMEM((2, 16, 8, 32, EMB), i16),
            pltpu.SemaphoreType.DMA((2, 2)),
        ],
        compiler_params=params(58),
        cost_estimate=cost(10**9, 80 * MIB),
        name="scatter",
    )(look, clash, flat, mine, bags, grads)


def split(values):
    high = values.astype(bf16)
    return high, (values - high.astype(f32)).astype(bf16)


def hidden_at(count, at):
    return count * 256 + at * 128


def out_at(count):
    return count * 384


def powers_at(count, s):
    return count * 384 + (16 if s == 0 else 0)


def powers_in(count):
    return 32 if count == 8 else 16


def put_hot(send_ref, power_ref, at, total):
    coded, power = code(total)
    rows = total.shape[0]
    send_ref[pl.ds(pl.multiple_of(at * 256, 256), rows), :] = coded
    for b in range(rows // 128):
        power_ref[pl.ds(at * 2 + b, 1), :] = power[b : b + 1]


def get_hot(recv_ref, power_ref, at, many):
    power = [power_ref[pl.ds(at * 2 + b, 1), :] for b in range(2 * many)]
    return decode_rows(
        recv_ref[pl.ds(pl.multiple_of(at * 256, 256), many * 256), :],
        jnp.concatenate(power, axis=0),
    )


def put_hidden(send_ref, power_ref, count, at, total):
    coded, power = code_twice(jnp.concatenate([total[:, :128], total[:, 128:]], axis=0))
    send_ref[hidden_at(count, at) : hidden_at(count, at) + 128, :] = coded
    power_ref[2 * count + at : 2 * count + at + 1, :] = power


def get_hidden(recv_ref, power_ref, count, at):
    both = decode_twice(
        recv_ref[hidden_at(count, at) : hidden_at(count, at) + 128, :],
        power_ref[2 * count + at : 2 * count + at + 1, :],
    )
    return jnp.concatenate([both[:32], both[32:]], axis=1)


def put_out(send_ref, power_ref, count, total):
    coded, power = code_twice(total)
    send_ref[out_at(count) : out_at(count) + 16, :] = coded
    power_ref[3 * count : 3 * count + 1, :] = power


def get_out(recv_ref, power_ref, count):
    return decode_twice(
        recv_ref[out_at(count) : out_at(count) + 16, :], power_ref[3 * count : 3 * count + 1, :]
    )


def put_powers(sends, power_ref, count):
    many = powers_in(count)
    for s in range(4):
        at = powers_at(count, s)
        power, bits = two_integers(power_ref[s, 0:many, :])
        sends[s][at : at + 2 * many, :] = whole(jnp.concatenate([power, bits], axis=0))


def get_powers(recvs, power_ref, count):
    many = powers_in(count)
    for s in range(4):
        at = powers_at(count, s)
        both = wide(recvs[s][at : at + 2 * many, :])
        power_ref[s, 0:many, :] = from_two(both[:many], both[many:])


def place_of(s, step, k):
    left = sorted(ORDERS[s][step:])
    bit = len(left) - 1 - left.index(ORDERS[s][step])
    rest = ((k >> (bit + 1)) << bit) | (k & ((1 << bit) - 1))
    return (k >> bit) & 1, rest


POWERS = pltpu.VMEM((4, 32, 128), f32)


def send_shapes(count):
    return tuple(
        shape((powers_at(count, s) + 2 * powers_in(count), EMB), i16) for s in range(4)
    ) + (shape((8, EMB), f32),)


def keep_shapes(count):
    return tuple(shape((count, 8, 32, EMB), f32) for s in range(4)) + tuple(
        shape((count, 32, 256), f32) for s in range(4)
    )


def core_sum(keep_ref, recv_ref, power_ref, s, k):
    power = [power_ref[pl.ds((s * 16 + k) * 2 + b, 1), :] for b in range(4)]
    coded = recv_ref[s, pl.ds(k, 2)].reshape(512, EMB)
    return keep_ref[s, pl.ds(k, 2)].reshape(512, EMB) + decode_rows(
        coded, jnp.concatenate(power, axis=0)
    )


def first_send_kernel(
    keep_ref, recv_ref, core_power_ref, hidden_ref, out_ref, out_recv_ref, *rest
):
    outs, power_ref = rest[:5], rest[5]
    power_ref[...] = jnp.zeros_like(power_ref)
    for s in range(4):

        def hot(k, _, s=s):
            total = core_sum(keep_ref, recv_ref, core_power_ref, s, 2 * k + 8)
            put_hot(outs[s], power_ref.at[s], 2 * k, total)
            return 0

        lax.fori_loop(0, 4, hot, 0)
        for k in range(16):
            flag, rest_at = place_of(s, 0, k)
            if flag:
                put_hidden(
                    outs[s],
                    power_ref.at[s],
                    8,
                    rest_at,
                    hidden_ref[32 * k : 32 * k + 32, 256 * s : 256 * s + 256],
                )
    total = out_ref[...] + out_recv_ref[...]
    outs[4][...] = total
    put_out(outs[0], power_ref.at[0], 8, total)
    put_powers(outs, power_ref, 8)


def first_send(keep, recv, power, hidden, out, out_recv):
    return pl.pallas_call(
        first_send_kernel,
        out_shape=send_shapes(8),
        in_specs=[VMEM] * 6,
        out_specs=[VMEM] * 5,
        scratch_shapes=[POWERS],
        compiler_params=params(24),
        cost_estimate=cost(10**6, 12 * MIB),
        name="first_send",
    )(keep, recv, power, hidden, out, out_recv)


def first_keep_kernel(keep_ref, recv_ref, core_power_ref, hidden_ref, *outs):
    for s in range(4):

        def hot(k, _, s=s):
            total = core_sum(keep_ref, recv_ref, core_power_ref, s, 2 * k)
            outs[s][pl.ds(2 * k, 2)] = total.reshape(2, 8, 32, EMB)
            return 0

        lax.fori_loop(0, 4, hot, 0)
        for k in range(16):
            flag, rest = place_of(s, 0, k)
            if not flag:
                outs[4 + s][rest] = hidden_ref[32 * k : 32 * k + 32, 256 * s : 256 * s + 256]


def first_keep(keep, recv, power, hidden):
    return pl.pallas_call(
        first_keep_kernel,
        out_shape=keep_shapes(8),
        in_specs=[VMEM] * 4,
        out_specs=[VMEM] * 8,
        compiler_params=params(24),
        cost_estimate=cost(10**6, 12 * MIB),
        name="first_keep",
    )(keep, recv, power, hidden)


def next_kernel(step, *refs):
    count = 16 >> step
    half = count // 2
    recvs, out_ref, hots, hiddens = refs[0:4], refs[4], refs[5:9], refs[9:13]
    sends, out_new_ref, hot_outs, hidden_outs = refs[13:17], refs[17], refs[18:22], refs[22:26]
    in_power_ref, power_ref = refs[26:]
    get_powers(recvs, in_power_ref, count)
    power_ref[...] = jnp.zeros_like(power_ref)
    for s in range(4):

        many = min(2, half)

        def hot(k, _, s=s, many=many):
            at = k * many
            rows = many * 256
            sums = [
                hots[s][pl.ds(first, many)].reshape(rows, EMB)
                + get_hot(recvs[s], in_power_ref.at[s], first, many)
                for first in (at + half, at)
            ]
            put_hot(sends[s], power_ref.at[s], at, sums[0])
            hot_outs[s][pl.ds(at, many)] = sums[1].reshape(many, 8, 32, EMB)
            return 0

        if half > many:
            lax.fori_loop(0, half // many, hot, 0)
        else:
            hot(0, 0)
        for k in range(count):
            flag, rest = place_of(s, step, k)
            hidden = hiddens[s][k] + get_hidden(recvs[s], in_power_ref.at[s], count, k)
            if flag:
                put_hidden(sends[s], power_ref.at[s], half, rest, hidden)
            else:
                hidden_outs[s][rest] = hidden
    total = out_ref[...] + get_out(recvs[0], in_power_ref.at[0], count)
    out_new_ref[...] = total
    put_out(sends[0], power_ref.at[0], half, total)
    put_powers(sends, power_ref, half)


def next_step(step, sends, keeps):
    count = 16 >> step
    values = pl.pallas_call(
        lambda *refs: next_kernel(step, *refs),
        out_shape=send_shapes(count // 2) + keep_shapes(count // 2),
        in_specs=[VMEM] * 13,
        out_specs=[VMEM] * 13,
        scratch_shapes=[POWERS, POWERS],
        compiler_params=params(24),
        cost_estimate=cost(10**6, count * 2 * MIB),
        name="step_" + str(step + 1),
    )(*sends, *keeps)
    return values[:5], values[5:]


AUX = 40
Z_ROWS = 128 + 2 * AUX + 16


def last_kernel(*refs):
    recvs, sum_ref, hots, hiddens, out_ref, pieces_ref, rows_ref, in_power_ref = (
        refs[0:4], refs[4], refs[5:9], refs[9:13], refs[13], refs[14], refs[15], refs[16],
    )
    get_powers(recvs, in_power_ref, 1)
    for s in range(4):
        total = hots[s][0].reshape(256, EMB) + get_hot(recvs[s], in_power_ref.at[s], 0, 1)
        hidden = hiddens[s][0] + get_hidden(recvs[s], in_power_ref.at[s], 1, 0)
        for z in range(8):
            rows_ref[z, 32 * s : 32 * s + 32, :] = total[32 * z : 32 * z + 32]
            for half in range(2):
                row = (2 * s + half) * 4
                pieces_ref[z, row : row + 4, :] = hidden[
                    4 * z : 4 * z + 4, half * 128 : half * 128 + 128
                ]
    total = sum_ref[...] + get_out(recvs[0], in_power_ref.at[0], 1)
    hot, powers = code(rows_ref[...].reshape(1024, EMB))
    for z in range(8):
        pieces_ref[z, 32:AUX, :] = total
        out_ref[z, 0:128, :] = hot[128 * z : 128 * z + 128]
        power = powers[z : z + 1]
        coded, aux_power = code_twice(pieces_ref[z])
        out_ref[z, 128 : 128 + 2 * AUX, :] = coded
        power, bits = two_integers(jnp.concatenate([power, aux_power], axis=0))
        out_ref[z, 128 + 2 * AUX :, :] = whole(
            jnp.concatenate([power, bits, jnp.zeros((12, 128), f32)], axis=0)
        )


def arrived(recv_ref):
    rows = jnp.zeros((128, EMB), f32)
    aux = jnp.zeros((AUX, EMB), f32)
    for z in range(8):
        powers = wide(recv_ref[z, 128 + 2 * AUX :, :])
        powers = from_two(powers[0:2], powers[2:4])
        rows = rows + decode_rows(recv_ref[z, 0:128, :], powers[0:1])
        aux = aux + decode_twice(recv_ref[z, 128 : 128 + 2 * AUX, :], powers[1:2])
    return rows, aux


def last_step(sends, keeps):
    return pl.pallas_call(
        last_kernel,
        out_shape=shape((8, Z_ROWS, EMB), i16),
        in_specs=[VMEM] * 13,
        out_specs=VMEM,
        scratch_shapes=[
            pltpu.VMEM((8, AUX, EMB), f32),
            pltpu.VMEM((8, 128, EMB), f32),
            POWERS,
        ],
        compiler_params=params(16),
        cost_estimate=cost(10**6, 2 * MIB),
        name="step_5",
    )(*sends, *keeps)


def row_update(param, accum_row, grad):
    turned = grad.T
    accum_new = accum_row + jnp.sum(turned * turned, axis=0, keepdims=True) * (1.0 / EMB)
    return param - (learn_rate * turned / jnp.sqrt(accum_new)).T, accum_new


def update_kernel(
    place_ref,
    recv_ref,
    slab_ref,
    accum_ref,
    weight_ref,
    hid_accum_ref,
    out_weight_ref,
    out_accum_ref,
    new_ref,
    accum_new_ref,
    weight_new_ref,
    hid_new_ref,
    out_new_ref,
    out_accum_new_ref,
    out_ref,
):
    rows, aux = arrived(recv_ref)
    new_ref[...], accum_new_ref[...] = row_update(
        slab_ref[...].astype(f32), accum_ref[...], rows
    )
    hidden = aux[0:32]
    for part in range(8):
        columns = slice(part * 128, part * 128 + 128)
        grad = hidden[part * 4 : part * 4 + 4]
        accum_new = hid_accum_ref[:, columns] + grad * grad
        hid_new_ref[:, columns] = accum_new
        weight_new_ref[:, columns] = weight_ref[:, columns] - learn_rate * grad / jnp.sqrt(accum_new)
    out_ref[...] = aux[32:AUX]
    row = out_ref[pl.ds(place_ref[1], 1), :]
    grad = pltpu.roll(row, place_ref[2], 1)[:, 0:4]
    accum_new = out_accum_ref[...] + grad * grad
    out_accum_new_ref[...] = accum_new
    out_new_ref[...] = out_weight_ref[...] - learn_rate * grad / jnp.sqrt(accum_new)


def update_owned(place, recv, slab, accum, weight, hid_accum, out_weight, out_accum):
    return pl.pallas_call(
        update_kernel,
        out_shape=(
            shape((128, EMB), f32),
            shape((1, 128), f32),
            shape((4, HID), f32),
            shape((4, HID), f32),
            shape((1, 4), f32),
            shape((1, 4), f32),
        ),
        in_specs=[SMEM] + [VMEM] * 7,
        out_specs=[VMEM] * 6,
        scratch_shapes=[pltpu.VMEM((8, EMB), f32)],
        compiler_params=params(16),
        name="update",
    )(place, recv, slab, accum, weight, hid_accum, out_weight, out_accum)


def cold_grad_kernel(asked_ref, incoming_ref, a_ref, b_ref):
    asked = asked_ref[...]
    incoming = incoming_ref[...]
    for part in range(8):
        total = mm(one_hot(256, 128, asked - part * 256), incoming).astype(bf16)
        if part < 4:
            a_ref[part * 256 : part * 256 + 256, :] = total
        else:
            b_ref[part * 256 - 1024 : part * 256 - 768, :] = total


def cold_grads(asked, incoming):
    return pl.pallas_call(
        cold_grad_kernel,
        out_shape=(shape((1024, EMB), bf16),) * 2,
        in_specs=[VMEM] * 2,
        out_specs=[VMEM] * 2,
        compiler_params=params(24),
        cost_estimate=cost(2 * 10**9, 4 * MIB),
        name="cold_grads",
    )(asked, incoming)


def pair_kernel(a, b, c, d, e_ref, f_ref):
    e_ref[...] = (a[...].astype(f32) + b[...].astype(f32)).astype(bf16)
    f_ref[...] = (c[...].astype(f32) + d[...].astype(f32)).astype(bf16)


def pair_sums(a, b, c, d):
    return pl.pallas_call(
        pair_kernel,
        out_shape=(shape((1024, EMB), bf16),) * 2,
        in_specs=[VMEM] * 4,
        out_specs=[VMEM] * 2,
        compiler_params=params(16),
        name="pair_sums",
    )(a, b, c, d)


def cold_update_kernel(a, b, c, d, table_ref, accum_ref, new_ref, accum_new_ref):
    for block in range(16):
        one, two = (a, b) if block < 8 else (c, d)
        at = slice((block % 8) * 128, (block % 8) * 128 + 128)
        rows = slice(block * 128, block * 128 + 128)
        grad = one[at, :].astype(f32) + two[at, :].astype(f32)
        new_ref[rows, :], accum_new_ref[block : block + 1, :] = row_update(
            table_ref[rows, :], accum_ref[block : block + 1, :], grad
        )


def update_cold(a, b, c, d, table, accum):
    return pl.pallas_call(
        cold_update_kernel,
        out_shape=(shape((R_OWN, EMB), f32), shape((R_OWN // 128, 128), f32)),
        in_specs=[VMEM] * 6,
        out_specs=[VMEM] * 2,
        compiler_params=params(16),
        name="cold_update",
    )(a, b, c, d, table, accum)


def dp_index(z, x, core):
    return (z * 4 + x) * 2 + core


def over_core(value):
    pairs = [
        (dp_index(z, x, core), dp_index(z, x, 1 - core))
        for z in range(8)
        for x in range(4)
        for core in range(2)
    ]
    return lax.ppermute(value, "dp", pairs)


def over_axis(value, axis):
    swap = (lambda i: 3 - i) if axis in (0, 2) else (lambda i: i ^ 1)
    if axis >= 2:
        return lax.ppermute(value, "rep", [(y, swap(y)) for y in range(4)])
    pairs = [
        (dp_index(z, x, core), dp_index(z, swap(x), core))
        for z in range(8)
        for x in range(4)
        for core in range(2)
    ]
    return lax.ppermute(value, "dp", pairs)


Z_GROUPS = [[dp_index(z, x, core) for z in range(8)] for x in range(4) for core in range(2)]


def over_z(value):
    return lax.all_to_all(
        value, "dp", split_axis=0, concat_axis=0, tiled=True, axis_index_groups=Z_GROUPS
    )


def on_device(
    hot_slab,
    hot_accum,
    cold_table,
    cold_accum,
    touched_owner,
    touched_row,
    lookup_index,
    bag_id,
    labels,
    w_hidden,
    hidden_accum,
    w_out,
    out_accum,
):
    dp = lax.axis_index("dp")
    y = lax.axis_index("rep")
    core, x = dp & 1, (dp >> 1) & 3
    position = dp * 4 + y
    bits = ((x ^ (x >> 1)) << 2) | (y ^ (y >> 1))
    place = jnp.stack([position * 128, position >> 5, (128 - (position & 31) * 4) & 127]).astype(i32)
    mine = jnp.stack([(core << 9) | (bits << 5), core, bits]).astype(i32)

    rows = LOOK // 128
    look_rows = lookup_index.reshape(rows, 128)
    bag_flat = bag_id.reshape(LOOK)
    bag_rows = bag_id.reshape(rows, 128)

    requests, pos = route(touched_owner.reshape(1, UNIQ), touched_row.reshape(1, UNIQ))
    pos_flat = pos.reshape(UNIQ)
    look_hot, clash = clashes(look_rows)
    look_flat, clash = look_hot.reshape(LOOK), clash.reshape(rows * FLAGS)
    count_a = slot_counts(bag_flat, look_rows, bag_rows)
    asked = lax.all_to_all(requests, "dp", split_axis=0, concat_axis=0, tiled=True)
    asked, count_a, mine, place, pos_flat = lax.optimization_barrier(
        (asked, count_a, mine, place, pos_flat)
    )
    found = found_rows(asked, cold_table)
    returned = lax.all_to_all(
        found.reshape(N_DP, CAP, EMB), "dp", split_axis=0, concat_axis=0, tiled=True
    ).reshape(SLOTS, EMB)
    pooled, count_b = pool_hot(bag_flat, look_flat, look_rows, bag_rows, hot_slab)
    pooled, count_b, asked_row = lax.optimization_barrier(
        (pooled, count_b, asked.reshape(1, SLOTS))
    )
    bag_grad, outgoing, factors, out_grad = layer(
        pos_flat,
        pooled,
        count_a,
        count_b,
        returned,
        labels.reshape(1, B_DEV),
        w_hidden,
        w_out.reshape(1, HID),
    )
    incoming = lax.all_to_all(
        outgoing.reshape(N_DP, CAP, EMB), "dp", split_axis=0, concat_axis=0, tiled=True
    ).reshape(SLOTS, EMB)
    other_factors = over_core(factors)
    out_grad = out_grad.reshape(8, EMB)
    out_recv = over_core(out_grad)
    keep, send, power = scatter_hot(look_flat, clash, bag_flat, mine, bag_rows, bag_grad)
    send, incoming, other_factors, out_recv = lax.optimization_barrier(
        (send, incoming, other_factors, out_recv)
    )
    recv, power = over_core(send), over_core(power)
    cold_a, cold_b = cold_grads(asked_row, incoming)
    recv_a, recv_b = over_axis(cold_a, 3), over_axis(cold_b, 2)
    hidden = hidden_half(mine, factors, other_factors)
    sends = first_send(keep, recv, power, hidden, out_grad, out_recv)
    recv_a, recv_b, *sends = lax.optimization_barrier((recv_a, recv_b, *sends))
    keeps = first_keep(keep, recv, power, hidden)
    for step in range(4):
        travelled = [over_axis(sends[s], ORDERS[s][step]) for s in range(4)] + [sends[4]]
        if step < 3:
            sends, keeps = next_step(step + 1, travelled, keeps)
    parts = last_step(travelled, keeps)
    pair_a, pair_b = pair_sums(cold_a, recv_a, cold_b, recv_b)
    parts, pair_a, pair_b = lax.optimization_barrier((parts, pair_a, pair_b))
    recv_a, recv_b = over_axis(pair_a, 2), over_axis(pair_b, 3)
    parts = over_z(parts)
    cold_new, cold_accum_new = update_cold(
        pair_a, recv_a, pair_b, recv_b, cold_table, cold_accum.reshape(R_OWN // 128, 128)
    )

    own_slab = lax.dynamic_slice_in_dim(hot_slab, position * 128, 128, 0)
    own_hidden = lax.dynamic_slice_in_dim(w_hidden, position * 4, 4, 0).astype(f32)
    own_out = lax.dynamic_slice_in_dim(w_out, position * 4, 4, 0)
    hot_new, hot_accum_new, hidden_new, hidden_accum_new, out_new, out_accum_new = update_owned(
        place,
        parts,
        own_slab,
        hot_accum.reshape(1, 128),
        own_hidden,
        hidden_accum,
        own_out.reshape(1, 4),
        out_accum.reshape(1, 4),
    )
    return (
        hot_new,
        hot_accum_new.reshape(128),
        cold_new,
        cold_accum_new.reshape(R_OWN),
        hidden_new,
        hidden_accum_new,
        out_new.reshape(4),
        out_accum_new.reshape(4),
    )


def solution(mesh):
    both = ("dp", "rep")
    in_specs = (
        P(),
        P(both),
        P("dp", None),
        P("dp"),
        P(both, None),
        P(both),
        P(both),
        P(both, None),
        P(both),
        P(),
        P(both, None),
        P(),
        P(both),
    )
    out_specs = (
        P(both, None),
        P(both),
        P("dp", None),
        P("dp"),
        P(both, None),
        P(both, None),
        P(both),
        P(both),
    )
    return jax.shard_map(
        on_device, mesh=mesh, in_specs=in_specs, out_specs=out_specs, check_vma=False
    )
```

```python
import jax
import jax.numpy as jnp
from jax import lax
from jax.experimental import pallas as pl
from jax.experimental.pallas import tpu as pltpu
from jax.sharding import PartitionSpec as P

learn_rate = 0.05
bf16 = jnp.bfloat16
f32 = jnp.float32
i32 = jnp.int32

EMB = 128
HOT = 32768
FEAT = 8
HID = 1024
B_DEV = 256
BAGS = 2048
LOOK = 8192
UNIQ = 1024
CAP = 48
R_OWN = 2048
N_DP = 64
SLOTS = N_DP * CAP
GROUP = 16
BLOCK = 256
WINDOW = BLOCK + 16
BLOCKS = LOOK // BLOCK
BATCH = 4
FLAGS = 128
ANY = FLAGS - 1
LAST_START = BAGS - WINDOW
CUT = 384
ONE = 32704.0
REST = 16384.0
i16 = jnp.int16
MIB = 1 << 20

ORDERS = ((3, 2, 1, 0), (2, 3, 0, 1), (1, 0, 3, 2), (0, 1, 2, 3))

SMEM = pl.BlockSpec(memory_space=pltpu.SMEM)
VMEM = pl.BlockSpec(memory_space=pltpu.VMEM)
HBM = pl.BlockSpec(memory_space=pltpu.HBM)


def params(mib):
    return pltpu.CompilerParams(vmem_limit_bytes=mib * MIB)


def cost(flops, data):
    return pl.CostEstimate(flops=flops, bytes_accessed=data, transcendentals=0)


def shape(dims, dtype):
    return jax.ShapeDtypeStruct(dims, dtype)


def mm(a, b):
    return jnp.dot(a, b, preferred_element_type=f32)


def mm_nt(a, b):
    return lax.dot_general(a, b, (((1,), (1,)), ((), ())), preferred_element_type=f32)


def mm_tn(a, b):
    return lax.dot_general(a, b, (((0,), (0,)), ((), ())), preferred_element_type=f32)


def route_kernel(owner_ref, row_ref, request_ref, pos_ref):
    owner = owner_ref[...]
    row = row_ref[...]
    member = lax.broadcasted_iota(i32, (N_DP, UNIQ), 0) == owner
    ones = member.astype(f32).astype(bf16)
    upper = lax.broadcasted_iota(i32, (UNIQ, UNIQ), 0) < lax.broadcasted_iota(
        i32, (UNIQ, UNIQ), 1
    )
    before = mm(ones, upper.astype(f32).astype(bf16))
    within = jnp.sum(jnp.where(member, before, 0.0), axis=0, keepdims=True).astype(i32)
    pos_ref[...] = owner * CAP + within
    place = (lax.broadcasted_iota(i32, (CAP, UNIQ), 0) == within).astype(f32).astype(bf16)
    high = jnp.where(member, (row >> 6).astype(f32), 0.0).astype(bf16)
    low = jnp.where(member, (row & 63).astype(f32), 0.0).astype(bf16)
    total = mm_nt(high, place) * 64.0 + mm_nt(low, place)
    request_ref[...] = total.astype(i32)


def route(owner, row):
    return pl.pallas_call(
        route_kernel,
        out_shape=(shape((N_DP, CAP), i32), shape((1, UNIQ), i32)),
        in_specs=[VMEM] * 2,
        out_specs=[VMEM] * 2,
        compiler_params=params(16),
        name="route",
    )(owner, row)


def clash_kernel(look_ref, hot_ref, clash_ref):
    rows = LOOK // 128
    lane = lax.broadcasted_iota(i32, (rows, 128), 1) & (GROUP - 1)
    look = look_ref[...]
    look = jnp.where(look < HOT, look, HOT + lane)
    hot_ref[...] = look
    clash = jnp.zeros((rows, 128), f32)
    for shift in range(1, GROUP):
        same = (look == pltpu.roll(look, shift, 1)) & (lane >= shift)
        clash = jnp.maximum(clash, same.astype(f32))
    group = lax.broadcasted_iota(i32, (128, FLAGS), 0) // GROUP
    column = lax.broadcasted_iota(i32, (128, FLAGS), 1)
    gather = (group == column) | (column == ANY)
    clash_ref[...] = mm(clash.astype(bf16), gather.astype(f32).astype(bf16)).astype(i32)


def clashes(look):
    return pl.pallas_call(
        clash_kernel,
        out_shape=(shape((LOOK // 128, 128), i32), shape((LOOK // 128, FLAGS), i32)),
        in_specs=[VMEM],
        out_specs=[VMEM] * 2,
        compiler_params=params(16),
        name="clashes",
    )(look)


def found_kernel(asked_ref, table_ref, found_ref, rows_ref):
    def body(owner, _):
        for j in range(CAP):
            rows_ref[pl.ds(owner * CAP + j, 1), :] = table_ref[pl.ds(asked_ref[owner, j], 1), :]
        return 0

    lax.fori_loop(0, N_DP, body, 0)
    found_ref[...] = rows_ref[...].astype(bf16)


def found_rows(asked, table):
    return pl.pallas_call(
        found_kernel,
        out_shape=shape((SLOTS, EMB), bf16),
        in_specs=[SMEM, VMEM],
        out_specs=VMEM,
        scratch_shapes=[pltpu.VMEM((SLOTS, EMB), f32)],
        compiler_params=params(16),
        name="found",
    )(asked, table)


def one_hot(height, middle, numbers):
    place = lax.broadcasted_iota(i32, (height, numbers.shape[1]), 0) - middle
    place = place.astype(f32).astype(bf16)
    inside = (numbers >= 0) & (numbers < height)
    named = jnp.where(inside, numbers - middle, -middle - 2).astype(f32).astype(bf16)
    return jnp.where(place == named, jnp.ones((), bf16), jnp.zeros((), bf16))


def bags_of(flat_ref, bag_ref, k):
    start = jnp.minimum((flat_ref[k * BLOCK] // 16) * 16, LAST_START)
    start = pl.multiple_of(start, 16)
    in_bag = [one_hot(WINDOW, WINDOW // 2, bag_ref[pl.ds(2 * k + j, 1), :] - start) for j in range(2)]
    return start, jnp.concatenate(in_bag, axis=1)


def count_slots(base, flat_ref, look_ref, bag_ref, acc_ref):
    acc_ref[...] = jnp.zeros_like(acc_ref)
    many = acc_ref.shape[1]

    def body(q, _):
        parts = []
        for b in range(BATCH):
            k = BATCH * q + b
            start, in_bag = bags_of(flat_ref, bag_ref, k)
            in_slot = []
            for j in range(2):
                slots = look_ref[pl.ds(2 * k + j, 1), :] - (HOT + base)
                pieces = [one_hot(128, 64, slots - at) for at in range(0, many, 128)]
                in_slot.append(jnp.concatenate(pieces, axis=0))
            in_slot = jnp.concatenate(in_slot, axis=1)
            parts.append((start, mm_nt(in_bag, in_slot).astype(bf16)))
        for start, part in parts:
            acc_ref[pl.ds(start, WINDOW), :] += part
        return 0

    lax.fori_loop(0, BLOCKS // BATCH, body, 0)


def counts_out(acc_ref, counts_ref, sems):
    return [
        pltpu.make_async_copy(
            acc_ref.at[pl.ds(c * 512, 512)], counts_ref.at[pl.ds(c * 512, 512)], sems.at[c]
        )
        for c in range(4)
    ]


def counts_kernel(flat_ref, look_ref, bag_ref, counts_ref, acc_ref, sems):
    count_slots(0, flat_ref, look_ref, bag_ref, acc_ref)
    copies = counts_out(acc_ref, counts_ref, sems)
    for copy in copies:
        copy.start()
    for copy in copies:
        copy.wait()


def slot_counts(flat, look, bags):
    return pl.pallas_call(
        counts_kernel,
        out_shape=shape((BAGS, CUT), bf16),
        in_specs=[SMEM, VMEM, VMEM],
        out_specs=HBM,
        scratch_shapes=[pltpu.VMEM((BAGS, CUT), bf16), pltpu.SemaphoreType.DMA((4,))],
        compiler_params=params(58),
        cost_estimate=cost(5 * 10**9, 8 * MIB),
        name="counts",
    )(flat, look, bags)


CHUNKS = 8


def pool_kernel(
    flat_ref,
    look_ref,
    raw_ref,
    bag_ref,
    slab_ref,
    pooled_ref,
    counts_ref,
    slab_vmem,
    table_ref,
    rows_ref,
    counts_vmem,
    sems,
    count_sems,
):
    height = HOT // CHUNKS

    def copy(c):
        rows = pl.ds(c * height, height)
        return pltpu.make_async_copy(slab_ref.at[rows], slab_vmem.at[rows], sems.at[c])

    for c in range(CHUNKS):
        copy(c).start()
    count_slots(CUT, flat_ref, raw_ref, bag_ref, counts_vmem)
    out_copies = counts_out(counts_vmem, counts_ref, count_sems)
    for out_copy in out_copies:
        out_copy.start()
    pooled_ref[...] = jnp.zeros_like(pooled_ref)
    table_ref[HOT:, :] = jnp.zeros((GROUP, EMB), f32)
    for c in range(CHUNKS):
        copy(c).wait()

        def widen(q, _, c=c):
            rows = pl.ds(pl.multiple_of(c * height + q * 512, 512), 512)
            table_ref[rows, :] = slab_vmem[rows, :].astype(f32)
            return 0

        lax.fori_loop(0, height // 512, widen, 0)

    def gather(q, _):
        for j in range(32):
            at = q * 32 + j
            rows_ref[pl.ds(at, 1), :] = table_ref[pl.ds(look_ref[at], 1), :]
        return 0

    lax.fori_loop(0, LOOK // 32, gather, 0)

    def batch(q, _):
        parts = []
        for j in range(BATCH):
            k = q * BATCH + j
            start, in_bag = bags_of(flat_ref, bag_ref, k)
            rows = rows_ref[pl.ds(pl.multiple_of(k * BLOCK, BLOCK), BLOCK), :].astype(bf16)
            parts.append((start, mm(in_bag, rows)))
        for start, part in parts:
            pooled_ref[pl.ds(start, WINDOW), :] += part
        return 0

    lax.fori_loop(0, BLOCKS // BATCH, batch, 0)
    for out_copy in out_copies:
        out_copy.wait()


def pool_hot(flat, look, raw, bags, slab):
    return pl.pallas_call(
        pool_kernel,
        out_shape=(shape((BAGS, EMB), f32), shape((BAGS, UNIQ - CUT), bf16)),
        in_specs=[SMEM, SMEM, VMEM, VMEM, HBM],
        out_specs=[VMEM, HBM],
        scratch_shapes=[
            pltpu.VMEM((HOT, EMB), bf16),
            pltpu.VMEM((HOT + GROUP, EMB), f32),
            pltpu.VMEM((LOOK, EMB), f32),
            pltpu.VMEM((BAGS, UNIQ - CUT), bf16),
            pltpu.SemaphoreType.DMA((CHUNKS,)),
            pltpu.SemaphoreType.DMA((4,)),
        ],
        compiler_params=params(58),
        cost_estimate=cost(10**9, 40 * MIB),
        name="pool",
    )(flat, look, raw, bags, slab)


def layer_kernel(
    pos_ref,
    pooled_ref,
    count_a_ref,
    count_b_ref,
    returned_ref,
    target_ref,
    weight_ref,
    out_weight_ref,
    bag_grad_ref,
    outgoing_ref,
    factors_ref,
    out_grad_ref,
    wide_ref,
    slots_ref,
    counts_vmem,
    weight_vmem,
    grads_vmem,
    factors_vmem,
    sems,
):
    counts_in = [
        pltpu.make_async_copy(count_a_ref, counts_vmem.at[:, pl.ds(0, CUT)], sems.at[0]),
        pltpu.make_async_copy(count_b_ref, counts_vmem.at[:, pl.ds(CUT, UNIQ - CUT)], sems.at[4]),
    ]
    weight_in = pltpu.make_async_copy(weight_ref, weight_vmem, sems.at[1])
    grads_out = pltpu.make_async_copy(grads_vmem, bag_grad_ref, sems.at[2])
    factors_out = pltpu.make_async_copy(factors_vmem, factors_ref, sems.at[3])
    for copy in counts_in:
        copy.start()
    weight_in.start()
    wide_ref[...] = returned_ref[...].astype(f32)

    def fetch(k, _):
        for j in range(16):
            at = k * 16 + j
            slots_ref[pl.ds(at, 1), :] = wide_ref[pl.ds(pos_ref[at], 1), :]
        return 0

    lax.fori_loop(0, UNIQ // 16, fetch, 0)
    for copy in counts_in:
        copy.wait()
    counts = counts_vmem[...]
    grads_vmem[...] = pooled_ref[...] + mm(counts, slots_ref[...].astype(bf16))
    pooled_in = jnp.concatenate(
        [grads_vmem[pl.ds(f, B_DEV, stride=FEAT), :] for f in range(FEAT)], axis=1
    ).astype(bf16)
    weight_in.wait()
    weight = weight_vmem[...]
    out_weight = out_weight_ref[...]
    preact = mm(pooled_in, weight)
    gate = jax.nn.sigmoid(preact)
    act = (preact * gate).astype(bf16).astype(f32)
    logits = jnp.sum(act * out_weight, axis=1, keepdims=True)
    diagonal = lax.broadcasted_iota(i32, (B_DEV, B_DEV), 0) == lax.broadcasted_iota(
        i32, (B_DEV, B_DEV), 1
    )
    target = jnp.sum(jnp.where(diagonal, target_ref[...], 0.0), axis=1, keepdims=True)
    logit_grad = jax.nn.sigmoid(logits) - target
    out_grad_ref[...] = jnp.sum(act * logit_grad, axis=0, keepdims=True)
    act_grad = (logit_grad * out_weight * gate * (1.0 + preact * (1.0 - gate))).astype(bf16)
    factors_vmem[0] = pooled_in
    factors_vmem[1] = act_grad
    factors_out.start()
    input_grad = mm_nt(act_grad, weight)
    for f in range(FEAT):
        grads_vmem[pl.ds(f, B_DEV, stride=FEAT), :] = input_grad[:, f * EMB : (f + 1) * EMB]

    grads_out.start()
    grads = grads_vmem[...]
    high = grads.astype(bf16)
    low = (grads - high.astype(f32)).astype(bf16)
    both = mm_tn(counts, jnp.concatenate([high, low], axis=1))
    slots_ref[...] = both[:, :EMB] + both[:, EMB:]
    wide_ref[...] = jnp.zeros_like(wide_ref)

    def put(k, _):
        for j in range(16):
            at = k * 16 + j
            wide_ref[pl.ds(pos_ref[at], 1), :] = slots_ref[pl.ds(at, 1), :]
        return 0

    lax.fori_loop(0, UNIQ // 16, put, 0)
    outgoing_ref[...] = wide_ref[...].astype(bf16)
    grads_out.wait()
    factors_out.wait()


def layer(pos, pooled, count_a, count_b, returned, target, weight, out_weight):
    return pl.pallas_call(
        layer_kernel,
        out_shape=(
            shape((BAGS, EMB), f32),
            shape((SLOTS, EMB), bf16),
            shape((2, B_DEV, HID), bf16),
            shape((1, HID), f32),
        ),
        in_specs=[SMEM, VMEM, HBM, HBM, VMEM, VMEM, HBM, VMEM],
        out_specs=[HBM, VMEM, HBM, VMEM],
        scratch_shapes=[
            pltpu.VMEM((SLOTS, EMB), f32),
            pltpu.VMEM((UNIQ, EMB), f32),
            pltpu.VMEM((BAGS, UNIQ), bf16),
            pltpu.VMEM((HID, HID), bf16),
            pltpu.VMEM((BAGS, EMB), f32),
            pltpu.VMEM((2, B_DEV, HID), bf16),
            pltpu.SemaphoreType.DMA((5,)),
        ],
        compiler_params=params(50),
        cost_estimate=cost(4 * 10**9, 20 * MIB),
        name="layer",
    )(pos, pooled, count_a, count_b, returned, target, weight, out_weight)


def hidden_kernel(mine_ref, one_ref, two_ref, hidden_ref):
    at = lax.broadcasted_iota(i32, (1, HID // 2), 1) ^ mine_ref[0]
    x_high, y_high = (at >> 8) & 1, (at >> 6) & 1
    x = 2 * x_high + (x_high ^ ((at >> 7) & 1))
    y = 2 * y_high + (y_high ^ ((at >> 5) & 1))
    source = ((((at >> 2) & 7) * 4 + x) * 2 + (at >> 9)) * 16 + y * 4 + (at & 3)
    order = (lax.broadcasted_iota(i32, (HID, HID // 2), 0) == source).astype(f32).astype(bf16)
    total = mm_tn(mm(one_ref[0], order).astype(bf16), one_ref[1])
    hidden_ref[...] = total + mm_tn(mm(two_ref[0], order).astype(bf16), two_ref[1])


def hidden_half(mine, one, two):
    return pl.pallas_call(
        hidden_kernel,
        out_shape=shape((HID // 2, HID), f32),
        in_specs=[SMEM, VMEM, VMEM],
        out_specs=VMEM,
        compiler_params=params(24),
        cost_estimate=cost(4 * 10**9, 4 * MIB),
        name="hidden_half",
    )(mine, one, two)


def diagonal(rows):
    return lax.broadcasted_iota(i32, (rows, 128), 0) == lax.broadcasted_iota(i32, (rows, 128), 1)


def blocks_of(values):
    rows = min(128, values.shape[0])
    return rows, range(values.shape[0] // rows)


def scales_of(values):
    rows = min(128, values.shape[0])
    most = jnp.maximum(jnp.max(jnp.abs(values), axis=1, keepdims=True), 1e-30)
    across = [
        jnp.sum(
            jnp.where(diagonal(rows), most[at : at + rows], 0.0), axis=0, keepdims=True
        )
        for at in range(0, values.shape[0], rows)
    ]
    return most, jnp.concatenate(across, axis=0)


def scaled(values, most):
    return values * (ONE / most)


def unscaled(values, across):
    blocks = across.shape[0]
    rows = values.shape[0] // blocks
    most = [
        jnp.sum(jnp.where(diagonal(rows), across[b : b + 1], 0.0), axis=1, keepdims=True)
        for b in range(blocks)
    ]
    return values * (jnp.concatenate(most, axis=0) * (1.0 / ONE))


def two_integers(across):
    power = jnp.floor(jnp.log(jnp.maximum(across, 1e-30)) * 1.4426950408889634) + 1.0
    return power, across * jnp.exp2(14.0 - power)


def from_two(power, bits):
    return bits * jnp.exp2(power - 14.0)


def nearest(values):
    return (values + 12582912.0) - 12582912.0


def whole(values):
    return nearest(values).astype(i32).astype(i16)


def wide(values):
    return values.astype(i32).astype(f32)


def code(values):
    most, across = scales_of(values)
    return whole(scaled(values, most)), across


def decode_rows(coded, across):
    return unscaled(wide(coded), across)


def code_twice(values):
    most, across = scales_of(values)
    values = scaled(values, most)
    high = nearest(values)
    return whole(jnp.concatenate([high, (values - high) * REST], axis=0)), across


def decode_twice(coded, across):
    coded = wide(coded)
    rows = coded.shape[0] // 2
    return unscaled(coded[:rows] + coded[rows:] * (1.0 / REST), across)


def scatter_kernel(
    look_ref,
    clash_ref,
    flat_ref,
    mine_ref,
    bag_ref,
    grad_ref,
    keep_ref,
    send_ref,
    power_ref,
    acc_ref,
    halves_ref,
    rows_ref,
    grad_vmem,
    keep_vmem,
    send_vmem,
    sems,
):
    grads_in = pltpu.make_async_copy(grad_ref, grad_vmem, sems.at[0, 0])
    grads_in.start()
    grads_in.wait()
    grads = grad_vmem[...]
    high, low = split(grads)
    halves_ref[:, 0:EMB] = high
    halves_ref[:, EMB:] = low

    def stage(q, _):
        for j in range(BATCH):
            k = q * BATCH + j
            start, in_bag = bags_of(flat_ref, bag_ref, k)
            both = mm_tn(in_bag, halves_ref[pl.ds(start, WINDOW), :])
            rows_ref[pl.ds(pl.multiple_of(k * BLOCK, BLOCK), BLOCK), :] = (
                both[:, :EMB] + both[:, EMB:]
            )
        acc_rows = HOT // (BLOCKS // BATCH)
        for j in range(acc_rows // 512):
            acc_ref[pl.ds(pl.multiple_of(q * acc_rows + j * 512, 512), 512), :] = jnp.zeros(
                (512, EMB), f32
            )
        return 0

    lax.fori_loop(0, BLOCKS // BATCH, stage, 0)

    def distinct(at):
        rows = [look_ref[at + m] for m in range(GROUP)]
        sums = [
            acc_ref[pl.ds(rows[m], 1), :] + rows_ref[pl.ds(at + m, 1), :] for m in range(GROUP)
        ]
        for m in range(GROUP):
            acc_ref[pl.ds(rows[m], 1), :] = sums[m]

    def block(k, _):
        clashes = clash_ref[k * FLAGS + ANY]

        @pl.when(clashes == 0)
        def _():
            def pair(q, _):
                distinct(k * 128 + q * 2 * GROUP)
                distinct(k * 128 + q * 2 * GROUP + GROUP)
                return 0

            lax.fori_loop(0, 128 // GROUP // 2, pair, 0)

        @pl.when(clashes != 0)
        def _():
            def group(q, _):
                at = k * 128 + q * GROUP
                clash = clash_ref[k * FLAGS + q]

                @pl.when(clash == 0)
                def _():
                    distinct(at)

                @pl.when(clash != 0)
                def _():
                    for m in range(GROUP):
                        acc_ref[pl.ds(look_ref[at + m], 1), :] += rows_ref[pl.ds(at + m, 1), :]

                return 0

            lax.fori_loop(0, 128 // GROUP, group, 0)

        return 0

    lax.fori_loop(0, LOOK // 128, block, 0)

    core, bits = mine_ref[1], mine_ref[2]

    def copies(s):
        return (
            pltpu.make_async_copy(send_vmem.at[s % 2], send_ref.at[s], sems.at[s % 2, 0]),
            pltpu.make_async_copy(keep_vmem.at[s % 2], keep_ref.at[s], sems.at[s % 2, 1]),
        )

    for s in range(4):
        if s >= 2:
            for copy in copies(s - 2):
                copy.wait()

        def gather(pair, _, s=s):
            rows = []
            for k in (4 * pair, 4 * pair + 1, 4 * pair + 2, 4 * pair + 3):
                bit = [(bits >> (3 - axis)) & 1 for axis in range(4)]
                for j, axis in enumerate(ORDERS[s]):
                    bit[axis] = bit[axis] ^ ((k >> (3 - j)) & 1)
                x = 2 * bit[0] + (bit[0] ^ bit[1])
                y = 2 * bit[2] + (bit[2] ^ bit[3])
                base = x * 1024 + y * 128 + 32 * s
                own = pl.multiple_of(base + 512 * core, 32)
                other = pl.multiple_of(base + 512 * (1 - core), 32)
                for z in range(8):
                    keep_vmem[s % 2, k, z] = acc_ref[pl.ds(own + z * 4096, 32), :]
                    rows.append(acc_ref[pl.ds(other + z * 4096, 32), :])
            coded, power = code(jnp.concatenate(rows, axis=0))
            send_vmem[s % 2, pl.ds(4 * pair, 4)] = coded.reshape(4, 8, 32, EMB)
            power_ref[pl.ds(pl.multiple_of((s * 4 + pair) * 8, 8), 8), :] = power
            return 0

        lax.fori_loop(0, 4, gather, 0)
        for copy in copies(s):
            copy.start()
    for s in (2, 3):
        for copy in copies(s):
            copy.wait()


def scatter_hot(look, clash, flat, mine, bags, grads):
    return pl.pallas_call(
        scatter_kernel,
        out_shape=(
            shape((4, 16, 8, 32, EMB), f32),
            shape((4, 16, 8, 32, EMB), i16),
            shape((128, 128), f32),
        ),
        in_specs=[SMEM] * 4 + [VMEM, HBM],
        out_specs=[HBM, HBM, VMEM],
        scratch_shapes=[
            pltpu.VMEM((HOT + GROUP, EMB), f32),
            pltpu.VMEM((BAGS, 2 * EMB), bf16),
            pltpu.VMEM((LOOK, EMB), f32),
            pltpu.VMEM((BAGS, EMB), f32),
            pltpu.VMEM((2, 16, 8, 32, EMB), f32),
            pltpu.VMEM((2, 16, 8, 32, EMB), i16),
            pltpu.SemaphoreType.DMA((2, 2)),
        ],
        compiler_params=params(58),
        cost_estimate=cost(10**9, 80 * MIB),
        name="scatter",
    )(look, clash, flat, mine, bags, grads)


def split(values):
    high = values.astype(bf16)
    return high, (values - high.astype(f32)).astype(bf16)


def hidden_rows(count):
    return slice(count * 256, count * 384)


def hidden_scales(count):
    return slice(2 * count, 2 * count + max(1, count // 2))


def out_at(count):
    return count * 384


def powers_at(count, s):
    return count * 384 + (16 if s == 0 else 0)


def powers_in(count):
    return 32 if count == 8 else 16


def put_hot(send_ref, power_ref, at, total):
    coded, power = code(total)
    rows = total.shape[0]
    send_ref[pl.ds(pl.multiple_of(at * 256, 256), rows), :] = coded
    for b in range(rows // 128):
        power_ref[pl.ds(at * 2 + b, 1), :] = power[b : b + 1]


def get_hot(recv_ref, power_ref, at, many):
    power = [power_ref[pl.ds(at * 2 + b, 1), :] for b in range(2 * many)]
    return decode_rows(
        recv_ref[pl.ds(pl.multiple_of(at * 256, 256), many * 256), :],
        jnp.concatenate(power, axis=0),
    )


def put_hidden(send_ref, power_ref, count, entries):
    rows = [half for total in entries for half in (total[:, :128], total[:, 128:])]
    coded, power = code_twice(jnp.concatenate(rows, axis=0))
    send_ref[hidden_rows(count), :] = coded
    power_ref[hidden_scales(count), :] = power


def get_hidden(recv_ref, power_ref, count):
    rows = decode_twice(recv_ref[hidden_rows(count), :], power_ref[hidden_scales(count), :])
    return [
        jnp.concatenate([rows[64 * at : 64 * at + 32], rows[64 * at + 32 : 64 * at + 64]], axis=1)
        for at in range(count)
    ]


def put_out(send_ref, power_ref, count, total):
    coded, power = code_twice(total)
    send_ref[out_at(count) : out_at(count) + 16, :] = coded
    power_ref[3 * count : 3 * count + 1, :] = power


def get_out(recv_ref, power_ref, count):
    return decode_twice(
        recv_ref[out_at(count) : out_at(count) + 16, :], power_ref[3 * count : 3 * count + 1, :]
    )


def put_powers(sends, power_ref, count):
    many = powers_in(count)
    for s in range(4):
        at = powers_at(count, s)
        power, bits = two_integers(power_ref[s, 0:many, :])
        sends[s][at : at + 2 * many, :] = whole(jnp.concatenate([power, bits], axis=0))


def get_powers(recvs, power_ref, count):
    many = powers_in(count)
    for s in range(4):
        at = powers_at(count, s)
        both = wide(recvs[s][at : at + 2 * many, :])
        power_ref[s, 0:many, :] = from_two(both[:many], both[many:])


def place_of(s, step, k):
    left = sorted(ORDERS[s][step:])
    bit = len(left) - 1 - left.index(ORDERS[s][step])
    rest = ((k >> (bit + 1)) << bit) | (k & ((1 << bit) - 1))
    return (k >> bit) & 1, rest


POWERS = pltpu.VMEM((4, 32, 128), f32)


def send_shapes(count):
    return tuple(
        shape((powers_at(count, s) + 2 * powers_in(count), EMB), i16) for s in range(4)
    ) + (shape((8, EMB), f32),)


def keep_shapes(count):
    return tuple(shape((count, 8, 32, EMB), f32) for s in range(4)) + tuple(
        shape((count, 32, 256), f32) for s in range(4)
    )


def core_sum(keep_ref, recv_ref, power_ref, s, k):
    power = power_ref[pl.ds(pl.multiple_of((s * 16 + k) * 2, 8), 8), :]
    coded = recv_ref[s, pl.ds(k, 4)].reshape(1024, EMB)
    return keep_ref[s, pl.ds(k, 4)].reshape(1024, EMB) + decode_rows(coded, power)


def first_send_kernel(
    keep_ref, recv_ref, core_power_ref, hidden_ref, out_ref, out_recv_ref, *rest
):
    outs, power_ref = rest[:5], rest[5]
    power_ref[...] = jnp.zeros_like(power_ref)
    for s in range(4):

        def hot(k, _, s=s):
            total = core_sum(keep_ref, recv_ref, core_power_ref, s, 4 * k + 8)
            put_hot(outs[s], power_ref.at[s], 4 * k, total)
            return 0

        lax.fori_loop(0, 2, hot, 0)
        entries = {}
        for k in range(16):
            flag, rest_at = place_of(s, 0, k)
            if flag:
                entries[rest_at] = hidden_ref[32 * k : 32 * k + 32, 256 * s : 256 * s + 256]
        put_hidden(outs[s], power_ref.at[s], 8, [entries[at] for at in range(8)])
    total = out_ref[...] + out_recv_ref[...]
    outs[4][...] = total
    put_out(outs[0], power_ref.at[0], 8, total)
    put_powers(outs, power_ref, 8)


def first_send(keep, recv, power, hidden, out, out_recv):
    return pl.pallas_call(
        first_send_kernel,
        out_shape=send_shapes(8),
        in_specs=[VMEM] * 6,
        out_specs=[VMEM] * 5,
        scratch_shapes=[POWERS],
        compiler_params=params(24),
        cost_estimate=cost(10**6, 12 * MIB),
        name="first_send",
    )(keep, recv, power, hidden, out, out_recv)


def first_keep_kernel(keep_ref, recv_ref, core_power_ref, hidden_ref, *outs):
    for s in range(4):

        def hot(k, _, s=s):
            total = core_sum(keep_ref, recv_ref, core_power_ref, s, 4 * k)
            outs[s][pl.ds(4 * k, 4)] = total.reshape(4, 8, 32, EMB)
            return 0

        lax.fori_loop(0, 2, hot, 0)
        for k in range(16):
            flag, rest = place_of(s, 0, k)
            if not flag:
                outs[4 + s][rest] = hidden_ref[32 * k : 32 * k + 32, 256 * s : 256 * s + 256]


def first_keep(keep, recv, power, hidden):
    return pl.pallas_call(
        first_keep_kernel,
        out_shape=keep_shapes(8),
        in_specs=[VMEM] * 4,
        out_specs=[VMEM] * 8,
        compiler_params=params(24),
        cost_estimate=cost(10**6, 12 * MIB),
        name="first_keep",
    )(keep, recv, power, hidden)


def next_kernel(step, *refs):
    count = 16 >> step
    half = count // 2
    recvs, out_ref, hots, hiddens = refs[0:4], refs[4], refs[5:9], refs[9:13]
    sends, out_new_ref, hot_outs, hidden_outs = refs[13:17], refs[17], refs[18:22], refs[22:26]
    in_power_ref, power_ref = refs[26:]
    get_powers(recvs, in_power_ref, count)
    power_ref[...] = jnp.zeros_like(power_ref)
    for s in range(4):

        many = min(4, half)

        def hot(k, _, s=s, many=many):
            at = k * many
            rows = many * 256
            sums = [
                hots[s][pl.ds(first, many)].reshape(rows, EMB)
                + get_hot(recvs[s], in_power_ref.at[s], first, many)
                for first in (at + half, at)
            ]
            put_hot(sends[s], power_ref.at[s], at, sums[0])
            hot_outs[s][pl.ds(at, many)] = sums[1].reshape(many, 8, 32, EMB)
            return 0

        if half > many:
            lax.fori_loop(0, half // many, hot, 0)
        else:
            hot(0, 0)
        entries = {}
        arrivals = get_hidden(recvs[s], in_power_ref.at[s], count)
        for k in range(count):
            flag, rest = place_of(s, step, k)
            hidden = hiddens[s][k] + arrivals[k]
            if flag:
                entries[rest] = hidden
            else:
                hidden_outs[s][rest] = hidden
        put_hidden(sends[s], power_ref.at[s], half, [entries[at] for at in range(half)])
    total = out_ref[...] + get_out(recvs[0], in_power_ref.at[0], count)
    out_new_ref[...] = total
    put_out(sends[0], power_ref.at[0], half, total)
    put_powers(sends, power_ref, half)


def next_step(step, sends, keeps):
    count = 16 >> step
    values = pl.pallas_call(
        lambda *refs: next_kernel(step, *refs),
        out_shape=send_shapes(count // 2) + keep_shapes(count // 2),
        in_specs=[VMEM] * 13,
        out_specs=[VMEM] * 13,
        scratch_shapes=[POWERS, POWERS],
        compiler_params=params(24),
        cost_estimate=cost(10**6, count * 2 * MIB),
        name="step_" + str(step + 1),
    )(*sends, *keeps)
    return values[:5], values[5:]


AUX = 40
Z_ROWS = 128 + 2 * AUX + 16


def last_kernel(*refs):
    recvs, sum_ref, hots, hiddens, out_ref, pieces_ref, rows_ref, in_power_ref = (
        refs[0:4], refs[4], refs[5:9], refs[9:13], refs[13], refs[14], refs[15], refs[16],
    )
    get_powers(recvs, in_power_ref, 1)
    for s in range(4):
        total = hots[s][0].reshape(256, EMB) + get_hot(recvs[s], in_power_ref.at[s], 0, 1)
        hidden = hiddens[s][0] + get_hidden(recvs[s], in_power_ref.at[s], 1)[0]
        for z in range(8):
            rows_ref[z, 32 * s : 32 * s + 32, :] = total[32 * z : 32 * z + 32]
            for half in range(2):
                row = (2 * s + half) * 4
                pieces_ref[z, row : row + 4, :] = hidden[
                    4 * z : 4 * z + 4, half * 128 : half * 128 + 128
                ]
    total = sum_ref[...] + get_out(recvs[0], in_power_ref.at[0], 1)
    hot, powers = code(rows_ref[...].reshape(1024, EMB))
    for z in range(8):
        pieces_ref[z, 32:AUX, :] = total
        out_ref[z, 0:128, :] = hot[128 * z : 128 * z + 128]
        power = powers[z : z + 1]
        coded, aux_power = code_twice(pieces_ref[z])
        out_ref[z, 128 : 128 + 2 * AUX, :] = coded
        power, bits = two_integers(jnp.concatenate([power, aux_power], axis=0))
        out_ref[z, 128 + 2 * AUX :, :] = whole(
            jnp.concatenate([power, bits, jnp.zeros((12, 128), f32)], axis=0)
        )


def arrived(recv_ref):
    rows = jnp.zeros((128, EMB), f32)
    aux = jnp.zeros((AUX, EMB), f32)
    for z in range(8):
        powers = wide(recv_ref[z, 128 + 2 * AUX :, :])
        powers = from_two(powers[0:2], powers[2:4])
        rows = rows + decode_rows(recv_ref[z, 0:128, :], powers[0:1])
        aux = aux + decode_twice(recv_ref[z, 128 : 128 + 2 * AUX, :], powers[1:2])
    return rows, aux


def last_step(sends, keeps):
    return pl.pallas_call(
        last_kernel,
        out_shape=shape((8, Z_ROWS, EMB), i16),
        in_specs=[VMEM] * 13,
        out_specs=VMEM,
        scratch_shapes=[
            pltpu.VMEM((8, AUX, EMB), f32),
            pltpu.VMEM((8, 128, EMB), f32),
            POWERS,
        ],
        compiler_params=params(16),
        cost_estimate=cost(10**6, 2 * MIB),
        name="step_5",
    )(*sends, *keeps)


def row_update(param, accum_row, grad):
    turned = grad.T
    accum_new = accum_row + jnp.sum(turned * turned, axis=0, keepdims=True) * (1.0 / EMB)
    return param - (learn_rate * turned / jnp.sqrt(accum_new)).T, accum_new


def update_kernel(
    place_ref,
    recv_ref,
    slab_ref,
    accum_ref,
    weight_ref,
    hid_accum_ref,
    out_weight_ref,
    out_accum_ref,
    new_ref,
    accum_new_ref,
    weight_new_ref,
    hid_new_ref,
    out_new_ref,
    out_accum_new_ref,
    out_ref,
):
    rows, aux = arrived(recv_ref)
    new_ref[...], accum_new_ref[...] = row_update(
        slab_ref[...].astype(f32), accum_ref[...], rows
    )
    hidden = aux[0:32]
    for part in range(8):
        columns = slice(part * 128, part * 128 + 128)
        grad = hidden[part * 4 : part * 4 + 4]
        accum_new = hid_accum_ref[:, columns] + grad * grad
        hid_new_ref[:, columns] = accum_new
        weight_new_ref[:, columns] = weight_ref[:, columns] - learn_rate * grad / jnp.sqrt(accum_new)
    out_ref[...] = aux[32:AUX]
    row = out_ref[pl.ds(place_ref[1], 1), :]
    grad = pltpu.roll(row, place_ref[2], 1)[:, 0:4]
    accum_new = out_accum_ref[...] + grad * grad
    out_accum_new_ref[...] = accum_new
    out_new_ref[...] = out_weight_ref[...] - learn_rate * grad / jnp.sqrt(accum_new)


def update_owned(place, recv, slab, accum, weight, hid_accum, out_weight, out_accum):
    return pl.pallas_call(
        update_kernel,
        out_shape=(
            shape((128, EMB), f32),
            shape((1, 128), f32),
            shape((4, HID), f32),
            shape((4, HID), f32),
            shape((1, 4), f32),
            shape((1, 4), f32),
        ),
        in_specs=[SMEM] + [VMEM] * 7,
        out_specs=[VMEM] * 6,
        scratch_shapes=[pltpu.VMEM((8, EMB), f32)],
        compiler_params=params(16),
        name="update",
    )(place, recv, slab, accum, weight, hid_accum, out_weight, out_accum)


def cold_grad_kernel(asked_ref, incoming_ref, a_ref, b_ref):
    asked = asked_ref[...]
    incoming = incoming_ref[...]
    for part in range(8):
        total = mm(one_hot(256, 128, asked - part * 256), incoming).astype(bf16)
        if part < 4:
            a_ref[part * 256 : part * 256 + 256, :] = total
        else:
            b_ref[part * 256 - 1024 : part * 256 - 768, :] = total


def cold_grads(asked, incoming):
    return pl.pallas_call(
        cold_grad_kernel,
        out_shape=(shape((1024, EMB), bf16),) * 2,
        in_specs=[VMEM] * 2,
        out_specs=[VMEM] * 2,
        compiler_params=params(24),
        cost_estimate=cost(2 * 10**9, 4 * MIB),
        name="cold_grads",
    )(asked, incoming)


def pair_kernel(a, b, c, d, e_ref, f_ref):
    e_ref[...] = (a[...].astype(f32) + b[...].astype(f32)).astype(bf16)
    f_ref[...] = (c[...].astype(f32) + d[...].astype(f32)).astype(bf16)


def pair_sums(a, b, c, d):
    return pl.pallas_call(
        pair_kernel,
        out_shape=(shape((1024, EMB), bf16),) * 2,
        in_specs=[VMEM] * 4,
        out_specs=[VMEM] * 2,
        compiler_params=params(16),
        name="pair_sums",
    )(a, b, c, d)


def cold_update_kernel(a, b, c, d, table_ref, accum_ref, new_ref, accum_new_ref):
    for block in range(16):
        one, two = (a, b) if block < 8 else (c, d)
        at = slice((block % 8) * 128, (block % 8) * 128 + 128)
        rows = slice(block * 128, block * 128 + 128)
        grad = one[at, :].astype(f32) + two[at, :].astype(f32)
        new_ref[rows, :], accum_new_ref[block : block + 1, :] = row_update(
            table_ref[rows, :], accum_ref[block : block + 1, :], grad
        )


def update_cold(a, b, c, d, table, accum):
    return pl.pallas_call(
        cold_update_kernel,
        out_shape=(shape((R_OWN, EMB), f32), shape((R_OWN // 128, 128), f32)),
        in_specs=[VMEM] * 6,
        out_specs=[VMEM] * 2,
        compiler_params=params(16),
        name="cold_update",
    )(a, b, c, d, table, accum)


def dp_index(z, x, core):
    return (z * 4 + x) * 2 + core


def over_core(value):
    pairs = [
        (dp_index(z, x, core), dp_index(z, x, 1 - core))
        for z in range(8)
        for x in range(4)
        for core in range(2)
    ]
    return lax.ppermute(value, "dp", pairs)


def over_axis(value, axis):
    swap = (lambda i: 3 - i) if axis in (0, 2) else (lambda i: i ^ 1)
    if axis >= 2:
        return lax.ppermute(value, "rep", [(y, swap(y)) for y in range(4)])
    pairs = [
        (dp_index(z, x, core), dp_index(z, swap(x), core))
        for z in range(8)
        for x in range(4)
        for core in range(2)
    ]
    return lax.ppermute(value, "dp", pairs)


Z_GROUPS = [[dp_index(z, x, core) for z in range(8)] for x in range(4) for core in range(2)]


def over_z(value):
    return lax.all_to_all(
        value, "dp", split_axis=0, concat_axis=0, tiled=True, axis_index_groups=Z_GROUPS
    )


def on_device(
    hot_slab,
    hot_accum,
    cold_table,
    cold_accum,
    touched_owner,
    touched_row,
    lookup_index,
    bag_id,
    labels,
    w_hidden,
    hidden_accum,
    w_out,
    out_accum,
):
    dp = lax.axis_index("dp")
    y = lax.axis_index("rep")
    core, x = dp & 1, (dp >> 1) & 3
    position = dp * 4 + y
    bits = ((x ^ (x >> 1)) << 2) | (y ^ (y >> 1))
    place = jnp.stack([position * 128, position >> 5, (128 - (position & 31) * 4) & 127]).astype(i32)
    mine = jnp.stack([(core << 9) | (bits << 5), core, bits]).astype(i32)

    rows = LOOK // 128
    look_rows = lookup_index.reshape(rows, 128)
    bag_flat = bag_id.reshape(LOOK)
    bag_rows = bag_id.reshape(rows, 128)

    requests, pos = route(touched_owner.reshape(1, UNIQ), touched_row.reshape(1, UNIQ))
    pos_flat = pos.reshape(UNIQ)
    look_hot, clash = clashes(look_rows)
    look_flat, clash = look_hot.reshape(LOOK), clash.reshape(rows * FLAGS)
    count_a = slot_counts(bag_flat, look_rows, bag_rows)
    asked = lax.all_to_all(requests, "dp", split_axis=0, concat_axis=0, tiled=True)
    asked, count_a, mine, place, pos_flat = lax.optimization_barrier(
        (asked, count_a, mine, place, pos_flat)
    )
    found = found_rows(asked, cold_table)
    returned = lax.all_to_all(
        found.reshape(N_DP, CAP, EMB), "dp", split_axis=0, concat_axis=0, tiled=True
    ).reshape(SLOTS, EMB)
    pooled, count_b = pool_hot(bag_flat, look_flat, look_rows, bag_rows, hot_slab)
    pooled, count_b, asked_row = lax.optimization_barrier(
        (pooled, count_b, asked.reshape(1, SLOTS))
    )
    bag_grad, outgoing, factors, out_grad = layer(
        pos_flat,
        pooled,
        count_a,
        count_b,
        returned,
        labels.reshape(1, B_DEV),
        w_hidden,
        w_out.reshape(1, HID),
    )
    incoming = lax.all_to_all(
        outgoing.reshape(N_DP, CAP, EMB), "dp", split_axis=0, concat_axis=0, tiled=True
    ).reshape(SLOTS, EMB)
    other_factors = over_core(factors)
    out_grad = out_grad.reshape(8, EMB)
    out_recv = over_core(out_grad)
    keep, send, power = scatter_hot(look_flat, clash, bag_flat, mine, bag_rows, bag_grad)
    send, incoming, other_factors, out_recv = lax.optimization_barrier(
        (send, incoming, other_factors, out_recv)
    )
    recv, power = over_core(send), over_core(power)
    cold_a, cold_b = cold_grads(asked_row, incoming)
    recv_a, recv_b = over_axis(cold_a, 3), over_axis(cold_b, 2)
    hidden = hidden_half(mine, factors, other_factors)
    sends = first_send(keep, recv, power, hidden, out_grad, out_recv)
    recv_a, recv_b, *sends = lax.optimization_barrier((recv_a, recv_b, *sends))
    keeps = first_keep(keep, recv, power, hidden)
    for step in range(4):
        travelled = [over_axis(sends[s], ORDERS[s][step]) for s in range(4)] + [sends[4]]
        if step < 3:
            sends, keeps = next_step(step + 1, travelled, keeps)
    parts = last_step(travelled, keeps)
    pair_a, pair_b = pair_sums(cold_a, recv_a, cold_b, recv_b)
    parts, pair_a, pair_b = lax.optimization_barrier((parts, pair_a, pair_b))
    recv_a, recv_b = over_axis(pair_a, 2), over_axis(pair_b, 3)
    parts = over_z(parts)
    cold_new, cold_accum_new = update_cold(
        pair_a, recv_a, pair_b, recv_b, cold_table, cold_accum.reshape(R_OWN // 128, 128)
    )

    own_slab = lax.dynamic_slice_in_dim(hot_slab, position * 128, 128, 0)
    own_hidden = lax.dynamic_slice_in_dim(w_hidden, position * 4, 4, 0).astype(f32)
    own_out = lax.dynamic_slice_in_dim(w_out, position * 4, 4, 0)
    hot_new, hot_accum_new, hidden_new, hidden_accum_new, out_new, out_accum_new = update_owned(
        place,
        parts,
        own_slab,
        hot_accum.reshape(1, 128),
        own_hidden,
        hidden_accum,
        own_out.reshape(1, 4),
        out_accum.reshape(1, 4),
    )
    return (
        hot_new,
        hot_accum_new.reshape(128),
        cold_new,
        cold_accum_new.reshape(R_OWN),
        hidden_new,
        hidden_accum_new,
        out_new.reshape(4),
        out_accum_new.reshape(4),
    )


def solution(mesh):
    both = ("dp", "rep")
    in_specs = (
        P(),
        P(both),
        P("dp", None),
        P("dp"),
        P(both, None),
        P(both),
        P(both),
        P(both, None),
        P(both),
        P(),
        P(both, None),
        P(),
        P(both),
    )
    out_specs = (
        P(both, None),
        P(both),
        P("dp", None),
        P("dp"),
        P(both, None),
        P(both, None),
        P(both),
        P(both),
    )
    return jax.shard_map(
        on_device, mesh=mesh, in_specs=in_specs, out_specs=out_specs, check_vma=False
    )
```
